128 devices in a mesh: row: 16 (over x, y), col: 8 (over z, core).
Axes of the slice: x: 4, y: 4, z: 4, core: 2. Of those that a mesh axis runs over, the one named last changes fastest.
Arguments:
- noise: float32 [320, 320, 320], P(None, 'row', 'col'), may hold values from -6 to 6
- owners: int32 [128, 800, 1], P(('row', 'col')), may hold values from 0 to 255; in each aligned block of 800 rows (0 to 799, 800 to 1599, ..., all dimensions but the last counted through in order) at most 4 rows name the same one
Outputs:
- arrived: float32 [128, 128, 2, 4, 3, 320], P(('row', 'col'))
The draws below stay inside these ranges and needn't reach their ends.
Inputs may be any that keep to these rules, and one draw needn't show every extreme that they name: `owners`: among the blocks of one device no domain appears more than 4 times, and in every draw some domain appears exactly 4 times among one device's blocks.
All inputs are finite; a program needn't handle non-finite values.
Results may differ from the reference program's by a relative error of at most 0.0001.
Values sent between devices are 32-bit elements; how exact they have to be, the bound alone decides.
No kernel may reach another device: no remote copies, remote signals or barrier semaphores. Data moves between devices by JAX's collectives and lax.ppermute only.
A program may use at most 128 MiB of HBM per device.

```python
import math
import jax
import jax.numpy as jnp
import numpy as np

GRID = 320
DOM_DEV = 2
CX = 20
CY = 40
DOMAINS = 256
DCAP = 4
N_ROW = 16
N_COL = 8


def block_levels(rng, dims, cuts, low, largest):
    def one(position, shards_of):
        steps = jax.random.uniform(jax.random.fold_in(jax.random.fold_in(rng, 6), position), (shards_of,), jnp.float32, low / len(cuts), largest / len(cuts))
        return jnp.repeat(jnp.exp(steps), dims[position] // shards_of).reshape((-1,) + (1,) * (len(dims) - position - 1))

    factor_of = one(*cuts[0])
    for cut in cuts[1:]:
        factor_of = factor_of * one(*cut)
    return factor_of


def shared_out(rng, own, number, rows, count, top, limit, slope):
    order = jax.random.permutation(rng, count)
    crowded, ordinary = shares(count, rows * top, limit, slope, True), shares(count, rows * top, limit, slope, False)
    places = jnp.arange(count)

    def named(tallies, rotation):
        used = int((tallies > 0).sum())
        fixed = max(1, used // 4)
        shifted = fixed + (places - fixed + rotation * (used - fixed)) % max(1, count - fixed)
        return jnp.zeros((count,), jnp.int32).at[order[jnp.where(places < fixed, places, shifted)]].set(jnp.asarray(tallies, jnp.int32))

    tallies = jnp.where(number % 4 == 0, named(crowded, number // 4), named(ordinary, number - number // 4 - 1))
    mixed = jax.random.permutation(jax.random.fold_in(own, 3), count)
    source_of, taker = mixed[0:count // 2 * 2:2], mixed[1:count // 2 * 2:2]
    margin = jnp.minimum(tallies[source_of] - 1, limit - tallies[taker]) // 2
    margin = jnp.where((source_of == order[0]) | (taker == order[0]) | (tallies[taker] == 0), 0, jnp.maximum(margin, 0))
    shifted = jax.random.randint(jax.random.fold_in(own, 4), (count // 2,), 0, 1 << 20) % (margin + 1)
    tallies = tallies.at[source_of].add(-shifted).at[taker].add(shifted)
    members = jnp.searchsorted(jnp.cumsum(tallies), jnp.arange(rows * top), side="right").astype(jnp.int32)
    grid = members.reshape(top, rows).T
    grid = grid[jax.random.permutation(jax.random.fold_in(own, 1), rows)]
    rotation = jax.random.randint(jax.random.fold_in(own, 2), (rows, 1), 0, top)
    return jnp.take_along_axis(grid, (jnp.arange(top)[None, :] + rotation) % top, axis=1)


def shares(count, total, reach, lean, full):
    loads = [(1 << 20) // math.isqrt(standing ** lean) + 1 for standing in range(1, count + 1)]
    largest = reach if full else min(reach, max(-(-total // count), total * loads[0] // sum(loads)))
    least = 1 if total - largest >= count - 1 else 0
    holding, spare = [largest] + [least] * (count - 1), total - largest - least * (count - 1)
    while spare > 0:
        movable = [i for i in range(1, count) if holding[i] < largest] or [i for i in range(1, count) if holding[i] < reach]
        mass, remaining = sum([loads[i] for i in movable]), spare
        for i in movable:
            addition = min(reach - holding[i], max(1, remaining * loads[i] // mass), spare)
            holding[i] = holding[i] + addition
            spare = spare - addition
    return np.array(holding)


def gaussian(stream_key, extent, spread, limit, pieces=(), kind=jnp.bfloat16):
    entries = spread * jax.random.normal(stream_key, extent, jnp.float32)
    if pieces:
        entries = entries * block_levels(stream_key, extent, pieces, -0.22, 0.18)
    return jnp.clip(entries, -limit, limit).astype(kind)


def setup_inputs(seed: int = 0) -> dict:
    key_list = jax.random.split(jax.random.key(seed), 3)
    noise = gaussian(key_list[0], (GRID, GRID, GRID), 1.0, 6.0, ((1, 16), (2, 8)), jnp.float32)
    owners_keys = jax.random.split(jax.random.fold_in(key_list[1], 1), (N_ROW * N_COL) * (CX * CY) // (CX * CY))
    owners_turns = jax.random.permutation(jax.random.fold_in(key_list[1], 3), (N_ROW * N_COL) * (CX * CY) // (CX * CY))
    owners = jax.vmap(lambda own, number: shared_out(jax.random.fold_in(key_list[1], 2), own, number, CX * CY, DOMAINS, 1, DCAP, 1))(owners_keys, owners_turns).reshape((N_ROW * N_COL, CX * CY, 1))
    return dict(noise=noise, owners=owners)


spectral_gain = 6.0


def wavenumber(index, total):
    signed = jnp.where(index < total // 2, index, index - total)
    return signed.astype(jnp.float32) * (2.0 * math.pi / total), index == total // 2


def kernel_of(kz, kx, ky, edge_z, edge_x, edge_y):
    ksquare = kx * kx + ky * ky + kz * kz
    edge = edge_z | edge_x | edge_y | (ksquare <= 0.0)
    safe = jnp.where(edge, 1.0, ksquare)
    return jnp.where(edge, 0.0, spectral_gain * safe ** -0.75 / (1.0 + safe))


def reference(noise, owners):
    index = jnp.arange(GRID, dtype=jnp.int32)
    kw, edge = wavenumber(index, GRID)
    kz = kw[:, None, None]
    kx = kw[None, :, None]
    ky = kw[None, None, :]
    kernel = kernel_of(kz, kx, ky, edge[:, None, None], edge[None, :, None], edge[None, None, :])
    spectrum = jnp.fft.fftn(noise)
    fields = []
    for wave in (kx, ky, kz):
        fields.append(jnp.real(jnp.fft.ifftn(1j * wave * kernel * spectrum)).astype(jnp.float32))
    psi = jnp.stack(fields)
    devices = N_ROW * N_COL
    blocks = psi.reshape(3, GRID, N_ROW, CX, N_COL, CY).transpose(2, 4, 3, 5, 0, 1)
    payload = blocks.reshape(devices, CX * CY, 3, GRID)
    owner = owners[:, :, 0]
    onehot = (owner[:, :, None] == jnp.arange(DOMAINS, dtype=jnp.int32)[None, None, :]).astype(jnp.int32)
    ranks = jnp.cumsum(onehot, axis=1) - 1
    slot = jnp.sum(ranks * onehot, axis=2)
    source = jnp.broadcast_to(jnp.arange(devices, dtype=jnp.int32)[:, None], owner.shape)
    arrived = jnp.zeros((devices, devices, DOM_DEV, DCAP, 3, GRID), jnp.float32)
    return arrived.at[owner // DOM_DEV, source, owner % DOM_DEV, slot].set(payload)
```

```python
import math

import jax
import jax.numpy as jnp
import ml_dtypes
import numpy as np
from jax import lax
from jax.experimental import pallas as pl
from jax.experimental.pallas import tpu as pltpu
from jax.sharding import Mesh
from jax.sharding import PartitionSpec as P

N = 320
GAIN = 6.0
ROWS, ZS, CORES = 16, 4, 2
CHIPS = ROWS * ZS
BU, BV = 20, 40
Q = 5
G = 7
LINES = BU * BV
EMPTY = G * 128
F32, BF16 = jnp.float32, jnp.bfloat16
STEP = 2.0 * math.pi / N


def basis():
    m = np.arange(N // 2)
    x = np.arange(N)
    angle = 2.0 * np.pi / N * (np.outer(m, x) % N)
    kw = (2.0 * np.pi / N * m)[:, None]
    weight = np.where(m == 0, 1.0, 2.0)[:, None] / N
    ana = np.zeros((N, N))
    syn = np.zeros((N, N))
    der = np.zeros((N, N))
    ana[0::2], ana[1::2] = np.cos(angle), np.sin(angle)
    syn[0::2], syn[1::2] = weight * np.cos(angle), weight * np.sin(angle)
    der[0::2], der[1::2] = -weight * kw * np.sin(angle), weight * kw * np.cos(angle)
    return ana, syn.T.copy(), der.T.copy()


def split_np(table):
    hi = table.astype(np.float32).astype(ml_dtypes.bfloat16)
    lo = (table - hi.astype(np.float64)).astype(np.float32).astype(ml_dtypes.bfloat16)
    return hi, lo


def lhs_table(table):
    hi, lo = split_np(table)
    return np.concatenate([hi, lo, hi], axis=1)


def rhs_table(table):
    hi, lo = split_np(table)
    return np.concatenate([hi, hi, lo], axis=0)


def make_tables():
    ana, syn, der = basis()
    third = np.arange(N)
    block, offset = third // BV, third % BV
    place = (block // 3) * 128 + (block % 3) * BV + offset
    first = ana.reshape(CHIPS, Q, N).transpose(1, 0, 2).reshape(N, N)
    t1 = np.zeros((384, 384))
    t1[place, :N] = ana.T
    a2 = np.zeros((N, 3, ROWS, 8))
    s3 = np.zeros((3, ROWS, G, N))
    d3 = np.zeros((3, ROWS, G, N))
    for i in range(3):
        for g in range(G):
            u = 3 * g + i
            if u < BU:
                at = np.arange(ROWS) * BU + u
                a2[:, i, :, g] = ana[:, at]
                s3[i, :, g] = syn[at]
                d3[i, :, g] = der[at]
    t4 = np.zeros((384, 384))
    t4[:N, place] = syn.T
    s5 = syn.reshape(N, CHIPS, Q).transpose(0, 2, 1).reshape(N, N)
    d5 = der.reshape(N, CHIPS, Q).transpose(0, 2, 1).reshape(N, N)
    m = np.arange(384) // 2
    kw = np.where(m < N // 2, 2.0 * np.pi / N * m, 0.0)
    even = np.arange(384) % 2 == 0
    swap = np.zeros((8, 384), np.float32)
    swap[0], swap[1] = np.where(even, kw, 0.0), np.where(even, 0.0, -kw)
    return dict(
        first=lhs_table(first),
        t1=rhs_table(t1),
        a2=lhs_table(a2.reshape(N, 384)),
        s3=lhs_table(s3.reshape(3 * ROWS * G, N)),
        d3=lhs_table(d3.reshape(3 * ROWS * G, N)),
        t4=rhs_table(t4),
        s5=lhs_table(s5),
        d5=lhs_table(d5),
        swap=swap,
    )


def split(value):
    hi = value.astype(BF16)
    return hi, (value - hi.astype(F32)).astype(BF16)


def rhs_split(value):
    hi, lo = split(value)
    return jnp.concatenate([hi, hi, lo], axis=0)


def lhs_split(value):
    hi, lo = split(value)
    return jnp.concatenate([hi, lo, hi], axis=1)


def dot(a, b):
    return jnp.dot(a, b, preferred_element_type=F32)


def dot_nt(a, b):
    return lax.dot_general(a, b, (((1,), (1,)), ((), ())), preferred_element_type=F32)


def column(row):
    return jnp.transpose(jnp.broadcast_to(row, (128, 128)))


def slot_codes(owner_ref):
    nb = 7
    lane = lax.broadcasted_iota(jnp.int32, (128, 128), 1)
    sub = lax.broadcasted_iota(jnp.int32, (128, 128), 0)
    one = lax.broadcasted_iota(jnp.int32, (1, 128), 1)
    rows = [owner_ref[:, b * 128 : (b + 1) * 128].astype(F32) for b in range(nb)]
    cols = [column(r) for r in rows]
    dests = []
    for b in range(nb):
        rank = jnp.sum(jnp.where((cols[b] == rows[b]) & (sub < lane), 1.0, 0.0), axis=0, keepdims=True)
        for e in range(b):
            rank = rank + jnp.sum(jnp.where(cols[e] == rows[b], 1.0, 0.0), axis=0, keepdims=True)
        owner = rows[b].astype(jnp.int32)
        device = owner >> 1
        dest = (device & 1) * (CHIPS * 8) + (device >> 1) * 8 + (owner & 1) * 4 + rank.astype(jnp.int32)
        dests.append(jnp.where(one + b * 128 < LINES, dest, -1).astype(F32))
    dcols = [column(d) for d in dests]
    values = []
    for b in range(nb):
        j = sub + b * 128
        group = jnp.zeros_like(j)
        for g in range(1, G):
            group = group + jnp.where(j >= g * 120, 1, 0)
        values.append((group * 8 + j - EMPTY).astype(F32))
    out = []
    for d in range(8):
        want = (lane + d * 128).astype(F32)
        total = jnp.zeros((128, 128), F32)
        for b in range(nb):
            total = total + jnp.where(dcols[b] == want, values[b], 0.0)
        out.append(jnp.sum(total, axis=0, keepdims=True) + float(EMPTY))
    return jnp.concatenate(out, axis=0)


def first_kernel(x_ref, owner_ref, table_ref, out_ref):
    codes = slot_codes(owner_ref)
    for j in range(CHIPS):
        out_ref[pl.ds(j * 48 + 40, 8), :] = codes
    parts = [x_ref[g * 120 : g * 120 + 128, :] for g in range(G - 1)]
    parts.append(x_ref[720:800, :])
    parts.append(jnp.zeros((48, N), F32))
    hi, lo = split(jnp.concatenate(parts, axis=0))
    th, tl = table_ref[:, 0:N], table_ref[:, N : 2 * N]
    y = dot_nt(th, hi) + (dot_nt(th, lo) + dot_nt(tl, hi))
    zero = jnp.zeros((CHIPS, 128), F32)
    for q in range(Q):
        for g in range(G):
            out_ref[pl.ds(q * 8 + g, CHIPS, stride=48), :] = y[q * CHIPS : (q + 1) * CHIPS, g * 128 : (g + 1) * 128]
        out_ref[pl.ds(q * 8 + G, CHIPS, stride=48), :] = zero


def middle_kernel(
    core_ref, own_ref, oth_ref, kern_ref, swap_ref, t1_ref, a2_ref, s3_ref, d3_ref, t4_ref,
    out_ref, u_ref, l4_ref, lines_ref, turn_ref,
):
    core = core_ref[0]
    mine = core == 0
    lane = lax.broadcasted_iota(jnp.int32, (1, 128), 1)

    pieces = []
    for z in range(ZS):
        a = own_ref[:, z, 0:40, :].reshape(ROWS * 40, 128)
        b = oth_ref[:, z, 0:40, :].reshape(ROWS * 40, 128)
        pieces.append(jnp.where(mine, a, b))
        pieces.append(jnp.where(mine, b, a))
    for i in range(3):
        cols = []
        for v in range(3):
            total = None
            for w in range(3):
                zc = 3 * v + w
                if zc >= 8:
                    continue
                shift = ((w - i) * BV) % 128
                moved = pltpu.roll(pieces[zc], shift, 1) if shift else pieces[zc]
                total = moved if total is None else jnp.where(lane >= w * BV, moved, total)
            cols.append(total)
        u_ref[i] = dot(lhs_split(jnp.concatenate(cols, axis=1)), t1_ref[...]).reshape(ROWS, Q, 8, 384)

    ca, cb = swap_ref[0:1, :], swap_ref[1:2, :]

    def plane(q, carry):
        parts = [u_ref[i, :, pl.ds(q, 1), :, :].reshape(ROWS * 8, 384) for i in range(3)]
        value = dot(a2_ref[...], rhs_split(jnp.concatenate(parts, axis=0))) * kern_ref[q]
        swapped = []
        for v in range(3):
            at = slice(v * 128, (v + 1) * 128)
            part = value[:, at]
            swapped.append(pltpu.roll(part, 127, 1) * ca[:, at] + pltpu.roll(part, 1, 1) * cb[:, at])
        plain = rhs_split(value)
        fields = (
            dot(d3_ref[...], plain),
            dot(s3_ref[...], rhs_split(jnp.concatenate(swapped, axis=1))),
            dot(s3_ref[...], plain),
        )
        for f in range(3):
            for i in range(3):
                for v in range(3):
                    part = fields[f][i * ROWS * G : (i + 1) * ROWS * G, v * 128 : (v + 1) * 128]
                    l4_ref[i, v, pl.ds(f * Q + q, ROWS * G, stride=16), :] = part
        return carry

    lax.fori_loop(0, Q, plane, 0)
    for i in range(3):
        for v in range(3):
            l4_ref[i, v, pl.ds(15, ROWS * G, stride=16), :] = jnp.zeros((ROWS * G, 128), F32)

    def rows4(r4, carry):
        ys = []
        for i in range(3):
            value = jnp.concatenate([l4_ref[i, v, pl.ds(r4 * 448, 448), :] for v in range(3)], axis=1)
            ys.append(dot(lhs_split(value), t4_ref[...]))
        for zc in range(8):
            v, w = zc // 3, zc % 3
            total = None
            for i in range(3):
                part = ys[i][:, v * 128 : (v + 1) * 128]
                shift = ((i - w) * BV) % 128
                part = pltpu.roll(part, shift, 1) if shift else part
                total = part if total is None else jnp.where(lane >= i * BV, part, total)
            lines_ref[zc] = total

        def one_row(rr, carry2):
            r = r4 * 4 + rr
            for zc in range(8):
                z, c = zc // 2, zc % 2
                blk = jnp.where(core == c, own_ref[r, z, 40:48, :], oth_ref[r, z, 40:48, :])
                code = jnp.where(mine, blk[0:4], blk[4:8]).astype(jnp.int32)
                for d in range(4):
                    idx = jnp.broadcast_to(code[d : d + 1], (16, 128))
                    at, group = idx & 127, idx >> 7
                    acc = jnp.zeros((16, 128), F32)
                    for g in range(G):
                        part = lines_ref[zc, pl.ds(rr * 112 + g * 16, 16), :]
                        acc = jnp.where(group == g, jnp.take_along_axis(part, at, axis=1), acc)
                    turn_ref[d, pl.ds(r * 8 + zc, 16, stride=128), :] = acc
            return carry2

        lax.fori_loop(0, 4, one_row, 0)
        return carry

    lax.fori_loop(0, 4, rows4, 0)

    def turned(pf, carry):
        for d in range(4):
            block = turn_ref[d, pl.ds(pf * 128, 128), :]
            out_ref[pl.ds(d * 2048 + pf, 128, stride=16), :] = jnp.transpose(block)
        return carry

    lax.fori_loop(0, 16, turned, 0)


def last_kernel(x_ref, s5_ref, d5_ref, out_ref):
    def load(slot, f):
        parts = [x_ref[pl.ds(slot * 16 + f * Q + q, CHIPS, stride=128), :] for q in range(Q)]
        return jnp.concatenate(parts, axis=0)

    def pair(k, carry):
        for e in range(2):
            slot = 2 * k + e
            both = rhs_split(jnp.concatenate([load(slot, 0), load(slot, 1)], axis=1))
            y = dot(s5_ref[...], both)
            out_ref[slot, 0] = y[:, 0:128]
            out_ref[slot, 1] = y[:, 128:256]
        both = rhs_split(jnp.concatenate([load(2 * k, 2), load(2 * k + 1, 2)], axis=1))
        y = dot(d5_ref[...], both)
        out_ref[2 * k, 2] = y[:, 0:128]
        out_ref[2 * k + 1, 2] = y[:, 128:256]
        return carry

    lax.fori_loop(0, 4, pair, 0)


VM = pl.BlockSpec(memory_space=pltpu.VMEM)
SM = pl.BlockSpec(memory_space=pltpu.SMEM)


def params(mib):
    return pltpu.CompilerParams(vmem_limit_bytes=mib * 2**20)


def first_call(x, owner, table):
    return pl.pallas_call(
        first_kernel,
        out_shape=jax.ShapeDtypeStruct((CHIPS * 48, 128), F32),
        in_specs=[VM] * 3,
        out_specs=VM,
        compiler_params=params(32),
    )(x, owner, table)


def middle_call(core, own, oth, kern, t):
    return pl.pallas_call(
        middle_kernel,
        out_shape=jax.ShapeDtypeStruct((CHIPS * 128, 128), F32),
        in_specs=[SM] + [VM] * 9,
        out_specs=VM,
        scratch_shapes=[
            pltpu.VMEM((3, ROWS, Q, 8, 384), F32),
            pltpu.VMEM((3, 3, ROWS * G * 16, 128), F32),
            pltpu.VMEM((8, 448, 128), F32),
            pltpu.VMEM((4, 16 * 128, 128), F32),
        ],
        compiler_params=params(56),
    )(core, own, oth, kern, t["swap"], t["t1"], t["a2"], t["s3"], t["d3"], t["t4"])


def last_call(x, s5, d5):
    return pl.pallas_call(
        last_kernel,
        out_shape=jax.ShapeDtypeStruct((8, 3, N, 128), F32),
        in_specs=[VM] * 3,
        out_specs=VM,
        compiler_params=params(32),
    )(x, s5, d5)


def filter_table(chip):
    def wave(p):
        return (p // 2).astype(F32) * STEP

    ka = wave(chip * Q + lax.iota(jnp.int32, Q))[:, None, None]
    kb = wave(lax.iota(jnp.int32, N))[None, :, None]
    kc = wave(lax.iota(jnp.int32, 384))[None, None, :]
    k2 = ka * ka + kb * kb + kc * kc
    off = (k2 <= 0.0) | (lax.iota(jnp.int32, 384)[None, None, :] >= N)
    safe = jnp.where(off, 1.0, k2)
    return jnp.where(off, 0.0, GAIN * safe ** (-0.75) / (1.0 + safe))


def local(noise, owners):
    t = make_tables()
    x = noise.transpose(1, 2, 0).reshape(LINES, N)
    owner = jnp.pad(owners.reshape(1, LINES), ((0, 0), (0, 896 - LINES)))
    sent = first_call(x, owner, t["first"]).reshape(CHIPS, 48, 128)
    own = lax.all_to_all(sent, ("row", "z"), split_axis=0, concat_axis=0, tiled=True)
    oth = lax.ppermute(own, "core", [(0, 1), (1, 0)])
    chip = lax.axis_index("row") * ZS + lax.axis_index("z")
    core = lax.axis_index("core").astype(jnp.int32).reshape(1)
    shape = (ROWS, ZS, 48, 128)
    slots = middle_call(core, own.reshape(shape), oth.reshape(shape), filter_table(chip), t)
    got = lax.all_to_all(slots.reshape(CHIPS, 128, 128), ("row", "z"), split_axis=0, concat_axis=0, tiled=True)
    out = last_call(got.reshape(CHIPS * 128, 128), t["s5"], t["d5"])
    return out.reshape(2, 4, 3, N, 128).transpose(4, 0, 1, 2, 3)[None]


def solution(mesh):
    fine = Mesh(mesh.devices.reshape(ROWS, ZS, CORES), ("row", "z", "core"))
    every = ("row", "z", "core")
    in_specs = (P(None, "row", ("z", "core")), P(every, None, None))
    out_specs = P(every, None, None, None, None, None)
    return jax.shard_map(local, mesh=fine, in_specs=in_specs, out_specs=out_specs, check_vma=False)
```

```python
import math

import jax
import jax.numpy as jnp
import ml_dtypes
import numpy as np
from jax import lax
from jax.experimental import pallas as pl
from jax.experimental.pallas import tpu as pltpu
from jax.sharding import Mesh
from jax.sharding import PartitionSpec as P

N = 320
GAIN = 6.0
ROWS, ZS, CORES = 16, 4, 2
CHIPS = ROWS * ZS
BU, BV = 20, 40
Q = 5
CH = 48
FQ = 3 * Q
G = 7
LINES = BU * BV
EMPTY = G * 128
F32, BF16 = jnp.float32, jnp.bfloat16
STEP = 2.0 * math.pi / N


def basis():
    m = np.arange(N // 2)
    x = np.arange(N)
    angle = 2.0 * np.pi / N * (np.outer(m, x) % N)
    kw = (2.0 * np.pi / N * m)[:, None]
    weight = np.where(m == 0, 1.0, 2.0)[:, None] / N
    ana = np.zeros((N, N))
    syn = np.zeros((N, N))
    der = np.zeros((N, N))
    ana[0::2], ana[1::2] = np.cos(angle), np.sin(angle)
    syn[0::2], syn[1::2] = weight * np.cos(angle), weight * np.sin(angle)
    der[0::2], der[1::2] = -weight * kw * np.sin(angle), weight * kw * np.cos(angle)
    return ana, syn.T.copy(), der.T.copy()


def split_np(table):
    hi = table.astype(np.float32).astype(ml_dtypes.bfloat16)
    lo = (table - hi.astype(np.float64)).astype(np.float32).astype(ml_dtypes.bfloat16)
    return hi, lo


def lhs_table(table):
    hi, lo = split_np(table)
    return np.concatenate([hi, lo, hi], axis=1)


def rhs_table(table):
    hi, lo = split_np(table)
    return np.concatenate([hi, hi, lo], axis=0)


def mix_table(table):
    hi, lo = split_np(table)
    return np.concatenate([hi[:256], hi[:256], lo[:256], hi[256:320], hi[256:320], lo[256:384]], axis=0)


def make_tables():
    ana, syn, der = basis()
    third = np.arange(N)
    block, offset = third // BV, third % BV
    places = [(block // 3) * 128 + ((block + i) % 3) * BV + offset for i in range(3)]
    first = ana.reshape(CHIPS, Q, N).transpose(1, 0, 2).reshape(N, N)
    t1 = np.zeros((3, 384, 384))
    t4 = np.zeros((3, 384, 384))
    for i in range(3):
        t1[i, places[i], :N] = ana.T
        t4[i][:N, places[i]] = syn.T
    a2 = np.zeros((N, 3, ROWS, 8))
    s3 = np.zeros((3, ROWS, 8, N))
    d3 = np.zeros((3, ROWS, 8, N))
    for i in range(3):
        for g in range(G):
            u = 3 * g + i
            if u < BU:
                at = np.arange(ROWS) * BU + u
                a2[:, i, :, g] = ana[:, at]
                s3[i, :, g] = syn[at]
                d3[i, :, g] = der[at]
    s5 = syn.reshape(N, CHIPS, Q).transpose(0, 2, 1).reshape(N, N)
    d5 = der.reshape(N, CHIPS, Q).transpose(0, 2, 1).reshape(N, N)
    m = np.arange(384) // 2
    kw = np.where(m < N // 2, 2.0 * np.pi / N * m, 0.0)
    even = np.arange(384) % 2 == 0
    swap = np.zeros((8, 384), np.float32)
    swap[0], swap[1] = np.where(even, kw, 0.0), np.where(even, 0.0, -kw)
    return dict(
        first=lhs_table(first),
        t1=np.stack([rhs_table(t) for t in t1]),
        a2=lhs_table(a2.reshape(N, 384)),
        s3=lhs_table(s3.reshape(384, N)),
        d3=lhs_table(d3.reshape(384, N)),
        t4=np.stack([mix_table(t) for t in t4]),
        s5=lhs_table(s5),
        d5=lhs_table(d5),
        swap=swap,
    )


def split(value):
    hi = value.astype(BF16)
    return hi, (value - hi.astype(F32)).astype(BF16)


def rhs_split(value):
    hi, lo = split(value)
    return jnp.concatenate([hi, hi, lo], axis=0)


def lhs_split(value):
    hi, lo = split(value)
    return jnp.concatenate([hi, lo, hi], axis=1)


def mix_split(value):
    hi, lo = split(value[:, :256])
    tail = value[:, 256:]
    tail_hi = tail.astype(BF16)
    moved = pltpu.roll(tail - tail_hi.astype(F32), 64, 1)
    lane = lax.broadcasted_iota(jnp.int32, (1, 128), 1)
    mixed = jnp.where(lane < 64, tail, moved).astype(BF16)
    return jnp.concatenate([hi, lo, hi, mixed, tail_hi], axis=1)


def dot(a, b):
    return jnp.dot(a, b, preferred_element_type=F32)


def dot_nt(a, b):
    return lax.dot_general(a, b, (((1,), (1,)), ((), ())), preferred_element_type=F32)


def column(row):
    return jnp.transpose(jnp.broadcast_to(row, (128, 128)))


def slot_codes(owner_ref, turn):
    nb = 7
    lane = lax.broadcasted_iota(jnp.int32, (128, 128), 1)
    sub = lax.broadcasted_iota(jnp.int32, (128, 128), 0)
    one = lax.broadcasted_iota(jnp.int32, (1, 128), 1)
    rows = [owner_ref[:, b * 128 : (b + 1) * 128].astype(F32) for b in range(nb)]
    cols = [column(r) for r in rows]
    dests = []
    for b in range(nb):
        rank = jnp.sum(jnp.where((cols[b] == rows[b]) & (sub < lane), 1.0, 0.0), axis=0, keepdims=True)
        for e in range(b):
            rank = rank + jnp.sum(jnp.where(cols[e] == rows[b], 1.0, 0.0), axis=0, keepdims=True)
        owner = rows[b].astype(jnp.int32)
        device = owner >> 1
        dest = (device & 1) * (CHIPS * 8) + (device >> 1) * 8 + (owner & 1) * 4 + rank.astype(jnp.int32)
        dests.append(jnp.where(one + b * 128 < LINES, dest, -1).astype(F32))
    dcols = [column(d) for d in dests]
    values = []
    for b in range(nb):
        j = sub + b * 128
        group = jnp.zeros_like(j)
        for g in range(1, G):
            group = group + jnp.where(j >= g * 120, 1, 0)
        place = j - group * 120 + turn * BV
        place = jnp.where(place >= 120, place - 120, place)
        values.append((group * 128 + place - EMPTY).astype(F32))
    out = []
    for d in range(8):
        want = (lane + d * 128).astype(F32)
        total = jnp.zeros((128, 128), F32)
        for b in range(nb):
            total = total + jnp.where(dcols[b] == want, values[b], 0.0)
        out.append(jnp.sum(total, axis=0, keepdims=True) + float(EMPTY))
    return jnp.concatenate(out, axis=0)


def first_kernel(turn_ref, x_ref, owner_ref, table_ref, out_ref):
    turn = turn_ref[0]
    codes = slot_codes(owner_ref, turn)
    for j in range(CHIPS):
        out_ref[pl.ds(j * 48 + 40, 8), :] = codes
    parts = []
    for g in range(G):
        for k in range(3):
            i = jnp.where(k >= turn, k - turn, k - turn + 3)
            u = g * 3 + i
            at = pl.multiple_of(jnp.minimum(u, BU - 1) * BV, 8)
            part = x_ref[pl.ds(at, BV), :]
            parts.append(part if g < G - 1 else jnp.where(u < BU, part, 0.0))
        parts.append(jnp.zeros((8, N), F32))
    hi, lo = split(jnp.concatenate(parts, axis=0))
    th, tl = table_ref[:, 0:N], table_ref[:, N : 2 * N]
    y = dot_nt(th, hi) + (dot_nt(th, lo) + dot_nt(tl, hi))
    zero = jnp.zeros((CHIPS, 128), F32)
    for q in range(Q):
        for g in range(G):
            out_ref[pl.ds(q * 8 + g, CHIPS, stride=48), :] = y[q * CHIPS : (q + 1) * CHIPS, g * 128 : (g + 1) * 128]
        out_ref[pl.ds(q * 8 + G, CHIPS, stride=48), :] = zero


def middle_kernel(
    core_ref, own_ref, oth_ref, kern_ref, swap_ref, t1_ref, a2_ref, s3_ref, d3_ref, t4_ref,
    out_ref, u_ref, l4_ref, even_ref, odd_ref, turn_ref, code_ref,
):
    core = core_ref[0]
    mine = core == 0
    lane = lax.broadcasted_iota(jnp.int32, (1, 128), 1)

    pieces = []
    for z in range(ZS):
        a = own_ref[:, z, 0:40, :].reshape(ROWS * 40, 128)
        b = oth_ref[:, z, 0:40, :].reshape(ROWS * 40, 128)
        pieces.append(jnp.where(mine, a, b))
        pieces.append(jnp.where(mine, b, a))
    for i in range(3):
        cols = []
        for v in range(3):
            part = [pieces[3 * v + (k - i) % 3] if 3 * v + (k - i) % 3 < 8 else None for k in range(3)]
            total = part[0] if part[0] is not None else part[1]
            for k in range(1, 3):
                if part[k] is not None and part[k] is not total:
                    total = jnp.where(lane >= k * BV, part[k], total)
            cols.append(total)
        u_ref[i] = dot(lhs_split(jnp.concatenate(cols, axis=1)), t1_ref[i]).reshape(ROWS, Q, 8, 384)

    ca, cb = swap_ref[0:1, :], swap_ref[1:2, :]

    def plane(q, carry):
        parts = [u_ref[i, :, pl.ds(q, 1), :, :].reshape(ROWS * 8, 384) for i in range(3)]
        value = dot(a2_ref[...], rhs_split(jnp.concatenate(parts, axis=0))) * kern_ref[q]
        swapped = []
        for v in range(3):
            at = slice(v * 128, (v + 1) * 128)
            part = value[:, at]
            swapped.append(pltpu.roll(part, 127, 1) * ca[:, at] + pltpu.roll(part, 1, 1) * cb[:, at])
        plain = rhs_split(value)
        fields = (
            dot(d3_ref[...], plain),
            dot(s3_ref[...], rhs_split(jnp.concatenate(swapped, axis=1))),
            dot(s3_ref[...], plain),
        )
        for f in range(3):
            for i in range(3):
                l4_ref[i, f * Q + q] = fields[f][i * 128 : (i + 1) * 128]
        return carry

    lax.fori_loop(0, Q, plane, 0)

    def sort_codes(r, carry):
        for zc in range(8):
            z, c = zc // 2, zc % 2
            blk = jnp.where(core == c, own_ref[r, z, 40:48, :], oth_ref[r, z, 40:48, :])
            code_ref[pl.ds(r * 32 + zc, 4, stride=8), :] = jnp.where(mine, blk[0:4], blk[4:8]).astype(jnp.int32)
        return carry

    lax.fori_loop(0, ROWS, sort_codes, 0)

    def lines_of(k, ref):
        at = pl.ds(pl.multiple_of(k * 16, 16), 16)
        ys = []
        for i in range(3):
            value = l4_ref[i, :, at, :].reshape(FQ * 16, 384)
            ys.append(dot(mix_split(value), t4_ref[i]).reshape(FQ, 16, 384))
            yield
        for zc in range(8):
            v, w = zc // 3, zc % 3
            total = None
            for k3 in range(3):
                part = ys[(k3 - w) % 3][:, :, v * 128 : (v + 1) * 128]
                total = part if total is None else jnp.where(lane >= k3 * BV, part, total)
            for rr in range(2):
                ref[rr, pl.ds(zc, FQ * 8, stride=8), :] = total[:, rr * 8 : rr * 8 + 8].reshape(FQ * 8, 128)
            if zc % 2:
                yield

    def pick(k, ref):
        for rr in range(2):
            for d in range(4):
                r = 2 * k + rr
                idx = code_ref[pl.ds(pl.multiple_of(r * 32 + d * 8, 8), 8), :]
                at, group = idx & 127, idx >> 7
                here = [group == g for g in range(G)]
                for pf in range(FQ):
                    acc = jnp.zeros((8, 128), F32)
                    for g in range(G):
                        part = ref[rr, (pf * 8 + g) * 8 : (pf * 8 + g) * 8 + 8, :]
                        acc = jnp.where(here[g], jnp.take_along_axis(part, at, axis=1), acc)
                    turn_ref[d, pl.ds(pl.multiple_of(pf * 128 + r * 8, 8), 8), :] = acc
                yield

    def together(*works):
        works = list(works)
        while works:
            works = [w for w in works if next(w, 0) is None]

    pairs = ROWS // 2
    together(lines_of(0, even_ref))

    def rows4(k, carry):
        together(lines_of(2 * k + 1, odd_ref), pick(2 * k, even_ref))
        together(lines_of(jnp.minimum(2 * k + 2, pairs - 1), even_ref), pick(2 * k + 1, odd_ref))
        return carry

    lax.fori_loop(0, pairs // 2, rows4, 0)

    def turned(pf, carry):
        for d in range(4):
            block = turn_ref[d, pl.ds(pf * 128, 128), :]
            out_ref[pl.ds(d * 128 * FQ + pf, 128, stride=FQ), :] = jnp.transpose(block)
        return carry

    lax.fori_loop(0, FQ, turned, 0)


def last_kernel(x_ref, s5_ref, d5_ref, out_ref):
    k = pl.program_id(0)

    def load(slot, f):
        parts = [x_ref[pl.ds(slot * FQ + f * Q + q, CHIPS, stride=8 * FQ), :] for q in range(Q)]
        return jnp.concatenate(parts, axis=0)

    for e in range(2):
        both = rhs_split(jnp.concatenate([load(2 * k + e, 0), load(2 * k + e, 1)], axis=1))
        y = dot(s5_ref[...], both)
        out_ref[e, 0] = y[:, 0:128]
        out_ref[e, 1] = y[:, 128:256]
    both = rhs_split(jnp.concatenate([load(2 * k, 2), load(2 * k + 1, 2)], axis=1))
    y = dot(d5_ref[...], both)
    out_ref[0, 2] = y[:, 0:128]
    out_ref[1, 2] = y[:, 128:256]


VM = pl.BlockSpec(memory_space=pltpu.VMEM)
SM = pl.BlockSpec(memory_space=pltpu.SMEM)


def params(mib):
    return pltpu.CompilerParams(vmem_limit_bytes=mib * 2**20)


def first_call(turn, x, owner, table):
    return pl.pallas_call(
        first_kernel,
        out_shape=jax.ShapeDtypeStruct((CHIPS * 48, 128), F32),
        in_specs=[SM] + [VM] * 3,
        out_specs=VM,
        compiler_params=params(32),
    )(turn, x, owner, table)


def middle_call(core, own, oth, kern, t):
    return pl.pallas_call(
        middle_kernel,
        out_shape=jax.ShapeDtypeStruct((CHIPS * 8 * FQ, 128), F32),
        in_specs=[SM] + [VM] * 9,
        out_specs=VM,
        scratch_shapes=[
            pltpu.VMEM((3, ROWS, Q, 8, 384), F32),
            pltpu.VMEM((3, FQ, 128, 384), F32),
            pltpu.VMEM((2, FQ * 64, 128), F32),
            pltpu.VMEM((2, FQ * 64, 128), F32),
            pltpu.VMEM((4, FQ * 128, 128), F32),
            pltpu.VMEM((ROWS * 32, 128), jnp.int32),
        ],
        compiler_params=params(40),
    )(core, own, oth, kern, t["swap"], t["t1"], t["a2"], t["s3"], t["d3"], t["t4"])


def last_call(x, s5, d5):
    return pl.pallas_call(
        last_kernel,
        grid=(4,),
        out_shape=jax.ShapeDtypeStruct((8, 3, N, 128), F32),
        in_specs=[VM] * 3,
        out_specs=pl.BlockSpec((2, 3, N, 128), lambda k: (k, 0, 0, 0)),
        compiler_params=params(32),
    )(x, s5, d5)


def filter_table(chip):
    def wave(p):
        return (p // 2).astype(F32) * STEP

    ka = wave(chip * Q + lax.iota(jnp.int32, Q))[:, None, None]
    kb = wave(lax.iota(jnp.int32, N))[None, :, None]
    kc = wave(lax.iota(jnp.int32, 384))[None, None, :]
    k2 = ka * ka + kb * kb + kc * kc
    off = (k2 <= 0.0) | (lax.iota(jnp.int32, 384)[None, None, :] >= N)
    safe = jnp.where(off, 1.0, k2)
    return jnp.where(off, 0.0, GAIN * safe ** (-0.75) / (1.0 + safe))


def local(noise, owners):
    t = make_tables()
    x = noise.transpose(1, 2, 0).reshape(LINES, N)
    owner = jnp.pad(owners.reshape(1, LINES), ((0, 0), (0, 896 - LINES)))
    core = lax.axis_index("core").astype(jnp.int32).reshape(1)
    turn = (lax.axis_index("z").astype(jnp.int32) * CORES + core) % 3
    sent = first_call(turn, x, owner, t["first"]).reshape(CHIPS, 48, 128)
    own = lax.all_to_all(sent, ("row", "z"), split_axis=0, concat_axis=0, tiled=True)
    oth = lax.ppermute(own, "core", [(0, 1), (1, 0)])
    chip = lax.axis_index("row") * ZS + lax.axis_index("z")
    shape = (ROWS, ZS, 48, 128)
    slots = middle_call(core, own.reshape(shape), oth.reshape(shape), filter_table(chip), t)
    got = lax.all_to_all(slots.reshape(CHIPS, 8 * FQ, 128), ("row", "z"), split_axis=0, concat_axis=0, tiled=True)
    out = last_call(got.reshape(CHIPS * 8 * FQ, 128), t["s5"], t["d5"])
    return out.reshape(2, 4, 3, N, 128).transpose(4, 0, 1, 2, 3)[None]


def solution(mesh):
    fine = Mesh(mesh.devices.reshape(ROWS, ZS, CORES), ("row", "z", "core"))
    every = ("row", "z", "core")
    in_specs = (P(None, "row", ("z", "core")), P(every, None, None))
    out_specs = P(every, None, None, None, None, None)
    return jax.shard_map(local, mesh=fine, in_specs=in_specs, out_specs=out_specs, check_vma=False)
```

```python
import math

import jax
import jax.numpy as jnp
import ml_dtypes
import numpy as np
from jax import lax
from jax.experimental import pallas as pl
from jax.experimental.pallas import tpu as pltpu
from jax.sharding import Mesh
from jax.sharding import PartitionSpec as P

N = 320
GAIN = 6.0
ROWS, ZS, CORES = 16, 4, 2
CHIPS = ROWS * ZS
BU, BV = 20, 40
Q = 5
CH = 48
FQ = 3 * Q
G = 7
LINES = BU * BV
EMPTY = G * 128
F32, BF16 = jnp.float32, jnp.bfloat16
STEP = 2.0 * math.pi / N


def basis():
    m = np.arange(N // 2)
    x = np.arange(N)
    angle = 2.0 * np.pi / N * (np.outer(m, x) % N)
    kw = (2.0 * np.pi / N * m)[:, None]
    weight = np.where(m == 0, 1.0, 2.0)[:, None] / N
    ana = np.zeros((N, N))
    syn = np.zeros((N, N))
    der = np.zeros((N, N))
    ana[0::2], ana[1::2] = np.cos(angle), np.sin(angle)
    syn[0::2], syn[1::2] = weight * np.cos(angle), weight * np.sin(angle)
    der[0::2], der[1::2] = -weight * kw * np.sin(angle), weight * kw * np.cos(angle)
    return ana, syn.T.copy(), der.T.copy()


def split_np(table):
    hi = table.astype(np.float32).astype(ml_dtypes.bfloat16)
    lo = (table - hi.astype(np.float64)).astype(np.float32).astype(ml_dtypes.bfloat16)
    return hi, lo


def lhs_table(table):
    hi, lo = split_np(table)
    return np.concatenate([hi, lo, hi], axis=1)


def rhs_table(table):
    hi, lo = split_np(table)
    return np.concatenate([hi, hi, lo], axis=0)


def mix_table(table):
    hi, lo = split_np(table)
    return np.concatenate([hi[:256], hi[:256], lo[:256], hi[256:320], hi[256:320], lo[256:384]], axis=0)


def make_tables():
    ana, syn, der = basis()
    third = np.arange(N)
    block, offset = third // BV, third % BV
    places = [(block // 3) * 128 + ((block + i) % 3) * BV + offset for i in range(3)]
    first = ana.reshape(CHIPS, Q, N).transpose(1, 0, 2).reshape(N, N)
    t1 = np.zeros((3, 384, 384))
    t4 = np.zeros((3, 384, 384))
    for i in range(3):
        t1[i, places[i], :N] = ana.T
        t4[i][:N, places[i]] = syn.T
    a2 = np.zeros((N, 3, ROWS, 8))
    s3 = np.zeros((3, ROWS, 8, N))
    d3 = np.zeros((3, ROWS, 8, N))
    for i in range(3):
        for g in range(G):
            u = 3 * g + i
            if u < BU:
                at = np.arange(ROWS) * BU + u
                a2[:, i, :, g] = ana[:, at]
                s3[i, :, g] = syn[at]
                d3[i, :, g] = der[at]
    s5 = syn.reshape(N, CHIPS, Q).transpose(0, 2, 1).reshape(N, N)
    d5 = der.reshape(N, CHIPS, Q).transpose(0, 2, 1).reshape(N, N)
    m = np.arange(384) // 2
    kw = np.where(m < N // 2, 2.0 * np.pi / N * m, 0.0)
    even = np.arange(384) % 2 == 0
    swap = np.zeros((8, 384), np.float32)
    swap[0], swap[1] = np.where(even, kw, 0.0), np.where(even, 0.0, -kw)
    def wide(table):
        table = np.pad(lhs_table(table), ((0, 0), (0, 1152)))
        return [table[:, k * 384 : (k + 1) * 384] for k in range(3)]

    blocks = [rhs_table(t) for t in t1]
    for table in (a2.reshape(N, 384), d3.reshape(384, N), s3.reshape(384, N)):
        blocks += wide(table)
    blocks += [mix_table(t) for t in t4]
    return dict(
        first=lhs_table(first),
        middle=np.concatenate(blocks, axis=0),
        s5=lhs_table(s5),
        d5=lhs_table(d5),
        swap=swap,
    )


def split(value):
    hi = value.astype(BF16)
    return hi, (value - hi.astype(F32)).astype(BF16)


def rhs_split(value):
    hi, lo = split(value)
    return jnp.concatenate([hi, hi, lo], axis=0)


def lhs_split(value):
    hi, lo = split(value)
    return jnp.concatenate([hi, lo, hi], axis=1)


def mix_split(value):
    hi, lo = split(value[:, :256])
    tail = value[:, 256:]
    tail_hi = tail.astype(BF16)
    moved = pltpu.roll(tail - tail_hi.astype(F32), 64, 1)
    lane = lax.broadcasted_iota(jnp.int32, (1, 128), 1)
    mixed = jnp.where(lane < 64, tail, moved).astype(BF16)
    return jnp.concatenate([hi, lo, hi, mixed, tail_hi], axis=1)


def dot(a, b):
    return jnp.dot(a, b, preferred_element_type=F32)


def dot_nt(a, b):
    return lax.dot_general(a, b, (((1,), (1,)), ((), ())), preferred_element_type=F32)


def column(row):
    return jnp.transpose(jnp.broadcast_to(row, (128, 128)))


def slot_codes(owner_ref, turn):
    nb = 7
    lane = lax.broadcasted_iota(jnp.int32, (128, 128), 1)
    sub = lax.broadcasted_iota(jnp.int32, (128, 128), 0)
    one = lax.broadcasted_iota(jnp.int32, (1, 128), 1)
    last = jnp.concatenate([owner_ref[:, 768:LINES], jnp.zeros((1, 896 - LINES), jnp.int32)], axis=1)
    rows = [(owner_ref[:, b * 128 : (b + 1) * 128] if b < nb - 1 else last).astype(F32) for b in range(nb)]
    cols = [column(r) for r in rows]
    dests = []
    for b in range(nb):
        rank = jnp.sum(jnp.where((cols[b] == rows[b]) & (sub < lane), 1.0, 0.0), axis=0, keepdims=True)
        for e in range(b):
            rank = rank + jnp.sum(jnp.where(cols[e] == rows[b], 1.0, 0.0), axis=0, keepdims=True)
        owner = rows[b].astype(jnp.int32)
        device = owner >> 1
        dest = (device & 1) * (CHIPS * 8) + (device >> 1) * 8 + (owner & 1) * 4 + rank.astype(jnp.int32)
        dests.append(jnp.where(one + b * 128 < LINES, dest, -1).astype(F32))
    dcols = [column(d) for d in dests]
    values = []
    for b in range(nb):
        j = sub + b * 128
        group = jnp.zeros_like(j)
        for g in range(1, G):
            group = group + jnp.where(j >= g * 120, 1, 0)
        place = j - group * 120 + turn * BV
        place = jnp.where(place >= 120, place - 120, place)
        values.append((group * 128 + place - EMPTY).astype(F32))
    out = []
    for d in range(8):
        want = (lane + d * 128).astype(F32)
        total = jnp.zeros((128, 128), F32)
        for b in range(nb):
            total = total + jnp.where(dcols[b] == want, values[b], 0.0)
        out.append(jnp.sum(total, axis=0, keepdims=True) + float(EMPTY))
    return jnp.concatenate(out, axis=0)


def first_kernel(turn_ref, x_hbm, owner_ref, table_hbm, out_ref, x_ref, table_ref, sems):
    copies = [
        pltpu.make_async_copy(x_hbm, x_ref, sems.at[0]),
        pltpu.make_async_copy(table_hbm, table_ref, sems.at[1]),
    ]
    for copy in copies:
        copy.start()
    turn = turn_ref[0]
    codes = slot_codes(owner_ref, turn)
    for j in range(CHIPS):
        out_ref[pl.ds(j * 48 + 40, 8), :] = codes
    for copy in copies:
        copy.wait()
    parts = []
    for g in range(G):
        for k in range(3):
            i = jnp.where(k >= turn, k - turn, k - turn + 3)
            u = g * 3 + i
            at = pl.multiple_of(jnp.minimum(u, BU - 1) * BV, 8)
            part = x_ref[pl.ds(at, BV), :]
            parts.append(part if g < G - 1 else jnp.where(u < BU, part, 0.0))
        parts.append(jnp.zeros((8, N), F32))
    hi, lo = split(jnp.concatenate(parts, axis=0))
    th, tl = table_ref[:, 0:N], table_ref[:, N : 2 * N]
    y = dot_nt(th, hi) + (dot_nt(th, lo) + dot_nt(tl, hi))
    zero = jnp.zeros((CHIPS, 128), F32)
    for q in range(Q):
        for g in range(G):
            out_ref[pl.ds(q * 8 + g, CHIPS, stride=48), :] = y[q * CHIPS : (q + 1) * CHIPS, g * 128 : (g + 1) * 128]
        out_ref[pl.ds(q * 8 + G, CHIPS, stride=48), :] = zero


def middle_kernel(
    core_ref, own_ref, oth_ref, kern_ref, swap_ref, table_hbm,
    out_ref, u_ref, l4_ref, even_ref, odd_ref, turn_ref, code_ref, t1_ref, a2_ref, d3_ref, s3_ref, t4_ref, sems,
):
    fetches = []
    row = 0
    targets = [t1_ref.at[i] for i in range(3)]
    for ref in (a2_ref, d3_ref, s3_ref):
        targets += [ref.at[:, k * 384 : (k + 1) * 384] for k in range(3)]
    targets += [t4_ref.at[i] for i in range(3)]
    for k, target in enumerate(targets):
        rows = target.shape[0]
        fetches.append(pltpu.make_async_copy(table_hbm.at[row : row + rows], target, sems.at[k]))
        fetches[-1].start()
        row += rows
    core = core_ref[0]
    mine = core == 0
    lane = lax.broadcasted_iota(jnp.int32, (1, 128), 1)

    pieces = []
    for z in range(ZS):
        a = own_ref[:, z, 0:40, :].reshape(ROWS * 40, 128)
        b = oth_ref[:, z, 0:40, :].reshape(ROWS * 40, 128)
        pieces.append(jnp.where(mine, a, b))
        pieces.append(jnp.where(mine, b, a))
    for i in range(3):
        cols = []
        for v in range(3):
            part = [pieces[3 * v + (k - i) % 3] if 3 * v + (k - i) % 3 < 8 else None for k in range(3)]
            total = part[0] if part[0] is not None else part[1]
            for k in range(1, 3):
                if part[k] is not None and part[k] is not total:
                    total = jnp.where(lane >= k * BV, part[k], total)
            cols.append(total)
        fetches[i].wait()
        u_ref[i] = dot(lhs_split(jnp.concatenate(cols, axis=1)), t1_ref[i]).reshape(ROWS, Q, 8, 384)

    ca, cb = swap_ref[0:1, :], swap_ref[1:2, :]

    def plane(q, carry):
        parts = [u_ref[i, :, pl.ds(q, 1), :, :].reshape(ROWS * 8, 384) for i in range(3)]
        value = dot(a2_ref[...], rhs_split(jnp.concatenate(parts, axis=0))) * kern_ref[q]
        swapped = []
        for v in range(3):
            at = slice(v * 128, (v + 1) * 128)
            part = value[:, at]
            swapped.append(pltpu.roll(part, 127, 1) * ca[:, at] + pltpu.roll(part, 1, 1) * cb[:, at])
        plain = rhs_split(value)
        fields = (
            dot(d3_ref[:, : 3 * N], plain),
            dot(s3_ref[:, : 3 * N], rhs_split(jnp.concatenate(swapped, axis=1))),
            dot(s3_ref[:, : 3 * N], plain),
        )
        for f in range(3):
            for i in range(3):
                l4_ref[i, f * Q + q] = fields[f][i * 128 : (i + 1) * 128]
        return carry

    for fetch in fetches[3:12]:
        fetch.wait()
    lax.fori_loop(0, Q, plane, 0, unroll=True)

    def sort_codes(r, carry):
        for zc in range(8):
            z, c = zc // 2, zc % 2
            blk = jnp.where(core == c, own_ref[r, z, 40:48, :], oth_ref[r, z, 40:48, :])
            code_ref[pl.ds(r * 32 + zc, 4, stride=8), :] = jnp.where(mine, blk[0:4], blk[4:8]).astype(jnp.int32)
        return carry

    lax.fori_loop(0, ROWS, sort_codes, 0)

    def lines_of(k, ref):
        at = pl.ds(pl.multiple_of(k * 16, 16), 16)
        ys = []
        for i in range(3):
            value = l4_ref[i, :, at, :].reshape(FQ * 16, 384)
            ys.append(dot(mix_split(value), t4_ref[i]).reshape(FQ, 16, 384))
            yield
        for zc in range(8):
            v, w = zc // 3, zc % 3
            total = None
            for k3 in range(3):
                part = ys[(k3 - w) % 3][:, :, v * 128 : (v + 1) * 128]
                total = part if total is None else jnp.where(lane >= k3 * BV, part, total)
            for rr in range(2):
                ref[rr, pl.ds(zc, FQ * 8, stride=8), :] = total[:, rr * 8 : rr * 8 + 8].reshape(FQ * 8, 128)
            if zc % 2:
                yield

    def pick(k, ref):
        for rr in range(2):
            for d in range(4):
                r = 2 * k + rr
                idx = code_ref[pl.ds(pl.multiple_of(r * 32 + d * 8, 8), 8), :]
                at, group = idx & 127, idx >> 7
                here = [group == g for g in range(G)]
                for pf in range(FQ):
                    acc = jnp.zeros((8, 128), F32)
                    for g in range(G):
                        part = ref[rr, (pf * 8 + g) * 8 : (pf * 8 + g) * 8 + 8, :]
                        acc = jnp.where(here[g], jnp.take_along_axis(part, at, axis=1), acc)
                    turn_ref[d, pl.ds(pl.multiple_of(pf * 128 + r * 8, 8), 8), :] = acc
                yield

    def together(*works):
        works = list(works)
        while works:
            works = [w for w in works if next(w, 0) is None]

    pairs = ROWS // 2
    for fetch in fetches[12:]:
        fetch.wait()
    together(lines_of(0, even_ref))

    def rows4(k, carry):
        together(lines_of(2 * k + 1, odd_ref), pick(2 * k, even_ref))
        together(lines_of(jnp.minimum(2 * k + 2, pairs - 1), even_ref), pick(2 * k + 1, odd_ref))
        return carry

    lax.fori_loop(0, pairs // 2, rows4, 0)

    def turned(pf, carry):
        for d in range(4):
            block = jnp.transpose(turn_ref[d, pl.ds(pl.multiple_of(pf * 128, 128), 128), :])
            for c in range(16):
                at = pl.multiple_of((d * 16 + c) * 8 * FQ + pf * 8, 8)
                out_ref[pl.ds(at, 8), :] = block[c * 8 : c * 8 + 8]
        return carry

    lax.fori_loop(0, FQ, turned, 0, unroll=5)


def last_kernel(x_ref, s5_ref, d5_ref, out_ref):
    k = pl.program_id(0)

    def load(slot, f):
        parts = [x_ref[pl.ds((f * Q + q) * 8 + slot, CHIPS, stride=8 * FQ), :] for q in range(Q)]
        return jnp.concatenate(parts, axis=0)

    for e in range(2):
        both = rhs_split(jnp.concatenate([load(2 * k + e, 0), load(2 * k + e, 1)], axis=1))
        y = dot(s5_ref[...], both)
        out_ref[e, 0] = y[:, 0:128]
        out_ref[e, 1] = y[:, 128:256]
    both = rhs_split(jnp.concatenate([load(2 * k, 2), load(2 * k + 1, 2)], axis=1))
    y = dot(d5_ref[...], both)
    out_ref[0, 2] = y[:, 0:128]
    out_ref[1, 2] = y[:, 128:256]


VM = pl.BlockSpec(memory_space=pltpu.VMEM)
SM = pl.BlockSpec(memory_space=pltpu.SMEM)
HB = pl.BlockSpec(memory_space=pltpu.HBM)


def params(mib):
    return pltpu.CompilerParams(vmem_limit_bytes=mib * 2**20)


def first_call(turn, x, owner, table):
    return pl.pallas_call(
        first_kernel,
        out_shape=jax.ShapeDtypeStruct((CHIPS * 48, 128), F32),
        in_specs=[SM, HB, VM, HB],
        out_specs=VM,
        scratch_shapes=[
            pltpu.VMEM(x.shape, F32),
            pltpu.VMEM(table.shape, BF16),
            pltpu.SemaphoreType.DMA((2,)),
        ],
        compiler_params=params(60),
    )(turn, x, owner, table)


def middle_call(core, own, oth, kern, t):
    shapes = ((3, 1152, 384), (N, 1152), (384, 1152), (384, 1152), (3, 1024, 384))
    return pl.pallas_call(
        middle_kernel,
        out_shape=jax.ShapeDtypeStruct((CHIPS * 8 * FQ, 128), F32),
        in_specs=[SM] + [VM] * 4 + [HB],
        out_specs=VM,
        scratch_shapes=[
            pltpu.VMEM((3, ROWS, Q, 8, 384), F32),
            pltpu.VMEM((3, FQ, 128, 384), F32),
            pltpu.VMEM((2, FQ * 64, 128), F32),
            pltpu.VMEM((2, FQ * 64, 128), F32),
            pltpu.VMEM((4, FQ * 128, 128), F32),
            pltpu.VMEM((ROWS * 32, 128), jnp.int32),
        ]
        + [pltpu.VMEM(shape, BF16) for shape in shapes]
        + [pltpu.SemaphoreType.DMA((15,))],
        compiler_params=params(42),
    )(core, own, oth, kern, t["swap"], t["middle"])


def last_call(x, s5, d5):
    return pl.pallas_call(
        last_kernel,
        grid=(4,),
        out_shape=jax.ShapeDtypeStruct((8, 3, N, 128), F32),
        in_specs=[VM] * 3,
        out_specs=pl.BlockSpec((2, 3, N, 128), lambda k: (k, 0, 0, 0)),
        compiler_params=params(32),
    )(x, s5, d5)


def filter_table(chip):
    def wave(p):
        return (p // 2).astype(F32) * STEP

    ka = wave(chip * Q + lax.iota(jnp.int32, Q))[:, None, None]
    kb = wave(lax.iota(jnp.int32, N))[None, :, None]
    kc = wave(lax.iota(jnp.int32, 384))[None, None, :]
    k2 = ka * ka + kb * kb + kc * kc
    off = (k2 <= 0.0) | (lax.iota(jnp.int32, 384)[None, None, :] >= N)
    safe = jnp.where(off, 1.0, k2)
    return jnp.where(off, 0.0, GAIN * safe ** (-0.75) / (1.0 + safe))


def local(noise, owners):
    t = make_tables()
    x = noise.transpose(1, 2, 0).reshape(LINES, N)
    owner = owners.reshape(1, LINES)
    core = lax.axis_index("core").astype(jnp.int32).reshape(1)
    turn = (lax.axis_index("z").astype(jnp.int32) * CORES + core) % 3
    sent = first_call(turn, x, owner, t["first"]).reshape(CHIPS, 48, 128)
    own = lax.all_to_all(sent, ("row", "z"), split_axis=0, concat_axis=0, tiled=True)
    oth = lax.ppermute(own, "core", [(0, 1), (1, 0)])
    chip = lax.axis_index("row") * ZS + lax.axis_index("z")
    shape = (ROWS, ZS, 48, 128)
    slots = middle_call(core, own.reshape(shape), oth.reshape(shape), filter_table(chip), t)
    got = lax.all_to_all(slots.reshape(CHIPS, 8 * FQ, 128), ("row", "z"), split_axis=0, concat_axis=0, tiled=True)
    out = last_call(got.reshape(CHIPS * 8 * FQ, 128), t["s5"], t["d5"])
    return out.reshape(2, 4, 3, N, 128).transpose(4, 0, 1, 2, 3)[None]


def solution(mesh):
    fine = Mesh(mesh.devices.reshape(ROWS, ZS, CORES), ("row", "z", "core"))
    every = ("row", "z", "core")
    in_specs = (P(None, "row", ("z", "core")), P(every, None, None))
    out_specs = P(every, None, None, None, None, None)
    return jax.shard_map(local, mesh=fine, in_specs=in_specs, out_specs=out_specs, check_vma=False)
```

```python
import math

import jax
import jax.numpy as jnp
import ml_dtypes
import numpy as np
from jax import lax
from jax.experimental import pallas as pl
from jax.experimental.pallas import tpu as pltpu
from jax.sharding import Mesh
from jax.sharding import PartitionSpec as P

N = 320
GAIN = 6.0
ROWS, ZS, CORES = 16, 4, 2
CHIPS = ROWS * ZS
BU, BV = 20, 40
Q = 5
CH = 48
FQ = 3 * Q
RR = 2
G = 7
LINES = BU * BV
EMPTY = G * 128
F32, BF16 = jnp.float32, jnp.bfloat16
STEP = 2.0 * math.pi / N


def basis():
    m = np.arange(N // 2)
    x = np.arange(N)
    angle = 2.0 * np.pi / N * (np.outer(m, x) % N)
    kw = (2.0 * np.pi / N * m)[:, None]
    weight = np.where(m == 0, 1.0, 2.0)[:, None] / N
    ana = np.zeros((N, N))
    syn = np.zeros((N, N))
    der = np.zeros((N, N))
    ana[0::2], ana[1::2] = np.cos(angle), np.sin(angle)
    syn[0::2], syn[1::2] = weight * np.cos(angle), weight * np.sin(angle)
    der[0::2], der[1::2] = -weight * kw * np.sin(angle), weight * kw * np.cos(angle)
    return ana, syn.T.copy(), der.T.copy()


def split_np(table):
    hi = table.astype(np.float32).astype(ml_dtypes.bfloat16)
    lo = (table - hi.astype(np.float64)).astype(np.float32).astype(ml_dtypes.bfloat16)
    return hi, lo


def lhs_table(table):
    hi, lo = split_np(table)
    return np.concatenate([hi, lo, hi], axis=1)


def rhs_table(table):
    hi, lo = split_np(table)
    return np.concatenate([hi, hi, lo], axis=0)


def mix_table(table):
    hi, lo = split_np(table)
    return np.concatenate([hi[:256], hi[:256], lo[:256], hi[256:320], hi[256:320], lo[256:384]], axis=0)


def make_tables():
    ana, syn, der = basis()
    third = np.arange(N)
    block, offset = third // BV, third % BV
    places = [(block // 3) * 128 + ((block + i) % 3) * BV + offset for i in range(3)]
    first = ana.reshape(CHIPS, Q, N).transpose(1, 0, 2).reshape(N, N)
    t1 = np.zeros((3, 384, 384))
    t4 = np.zeros((3, 384, 384))
    for i in range(3):
        t1[i, places[i], :N] = ana.T
        t4[i][:N, places[i]] = syn.T
    a2 = np.zeros((N, 3, ROWS, 8))
    s3 = np.zeros((3, ROWS, 8, N))
    d3 = np.zeros((3, ROWS, 8, N))
    for i in range(3):
        for g in range(G):
            u = 3 * g + i
            if u < BU:
                at = np.arange(ROWS) * BU + u
                a2[:, i, :, g] = ana[:, at]
                s3[i, :, g] = syn[at]
                d3[i, :, g] = der[at]
    s5 = syn.reshape(N, CHIPS, Q).transpose(0, 2, 1).reshape(N, N)
    d5 = der.reshape(N, CHIPS, Q).transpose(0, 2, 1).reshape(N, N)
    m = np.arange(384) // 2
    kw = np.where(m < N // 2, 2.0 * np.pi / N * m, 0.0)
    even = np.arange(384) % 2 == 0
    swap = np.zeros((8, 384), np.float32)
    swap[0], swap[1] = np.where(even, kw, 0.0), np.where(even, 0.0, -kw)
    def wide(table):
        table = np.pad(lhs_table(table), ((0, 0), (0, 1152)))
        return [table[:, k * 384 : (k + 1) * 384] for k in range(3)]

    blocks = [rhs_table(t) for t in t1]
    for table in (a2.reshape(N, 384), d3.reshape(384, N), s3.reshape(384, N)):
        blocks += wide(table)
    blocks += [mix_table(t) for t in t4]
    return dict(
        first=lhs_table(first),
        middle=np.concatenate(blocks, axis=0),
        s5=lhs_table(s5),
        d5=lhs_table(d5),
        swap=swap,
    )


def split(value):
    hi = value.astype(BF16)
    return hi, (value - hi.astype(F32)).astype(BF16)


def rhs_split(value):
    hi, lo = split(value)
    return jnp.concatenate([hi, hi, lo], axis=0)


def lhs_split(value):
    hi, lo = split(value)
    return jnp.concatenate([hi, lo, hi], axis=1)


def mix_split(value):
    hi, lo = split(value[:, :256])
    tail = value[:, 256:]
    tail_hi = tail.astype(BF16)
    moved = pltpu.roll(tail - tail_hi.astype(F32), 64, 1)
    lane = lax.broadcasted_iota(jnp.int32, (1, 128), 1)
    mixed = jnp.where(lane < 64, tail, moved).astype(BF16)
    return jnp.concatenate([hi, lo, hi, mixed, tail_hi], axis=1)


def dot(a, b):
    return jnp.dot(a, b, preferred_element_type=F32)


def dot_nt(a, b):
    return lax.dot_general(a, b, (((1,), (1,)), ((), ())), preferred_element_type=F32)


def column(row):
    return jnp.transpose(jnp.broadcast_to(row, (128, 128)))


def slot_codes(owner_ref, turn):
    nb = 7
    lane = lax.broadcasted_iota(jnp.int32, (128, 128), 1)
    sub = lax.broadcasted_iota(jnp.int32, (128, 128), 0)
    one = lax.broadcasted_iota(jnp.int32, (1, 128), 1)
    last = jnp.concatenate([owner_ref[:, 768:LINES], jnp.zeros((1, 896 - LINES), jnp.int32)], axis=1)
    rows = [(owner_ref[:, b * 128 : (b + 1) * 128] if b < nb - 1 else last).astype(F32) for b in range(nb)]
    cols = [column(r) for r in rows]
    dests = []
    for b in range(nb):
        rank = jnp.sum(jnp.where((cols[b] == rows[b]) & (sub < lane), 1.0, 0.0), axis=0, keepdims=True)
        for e in range(b):
            rank = rank + jnp.sum(jnp.where(cols[e] == rows[b], 1.0, 0.0), axis=0, keepdims=True)
        owner = rows[b].astype(jnp.int32)
        device = owner >> 1
        dest = (device & 1) * (CHIPS * 8) + (device >> 1) * 8 + (owner & 1) * 4 + rank.astype(jnp.int32)
        dests.append(jnp.where(one + b * 128 < LINES, dest, -1).astype(F32))
    dcols = [column(d) for d in dests]
    values = []
    for b in range(nb):
        j = sub + b * 128
        group = jnp.zeros_like(j)
        for g in range(1, G):
            group = group + jnp.where(j >= g * 120, 1, 0)
        place = j - group * 120 + turn * BV
        place = jnp.where(place >= 120, place - 120, place)
        values.append((group * 128 + place - EMPTY).astype(F32))
    out = []
    for d in range(8):
        want = (lane + d * 128).astype(F32)
        total = jnp.zeros((128, 128), F32)
        for b in range(nb):
            total = total + jnp.where(dcols[b] == want, values[b], 0.0)
        out.append(jnp.sum(total, axis=0, keepdims=True) + float(EMPTY))
    return jnp.concatenate(out, axis=0)


def first_kernel(turn_ref, x_hbm, owner_ref, table_hbm, out_ref, x_ref, table_ref, sems):
    copies = [
        pltpu.make_async_copy(x_hbm, x_ref, sems.at[0]),
        pltpu.make_async_copy(table_hbm, table_ref, sems.at[1]),
    ]
    for copy in copies:
        copy.start()
    turn = turn_ref[0]
    codes = slot_codes(owner_ref, turn)
    for j in range(CHIPS):
        out_ref[pl.ds(j * 48 + 40, 8), :] = codes
    for copy in copies:
        copy.wait()
    parts = []
    for g in range(G):
        for k in range(3):
            i = jnp.where(k >= turn, k - turn, k - turn + 3)
            u = g * 3 + i
            at = pl.multiple_of(jnp.minimum(u, BU - 1) * BV, 8)
            part = x_ref[pl.ds(at, BV), :]
            parts.append(part if g < G - 1 else jnp.where(u < BU, part, 0.0))
        parts.append(jnp.zeros((8, N), F32))
    hi, lo = split(jnp.concatenate(parts, axis=0))
    th, tl = table_ref[:, 0:N], table_ref[:, N : 2 * N]
    y = dot_nt(th, hi) + (dot_nt(th, lo) + dot_nt(tl, hi))
    zero = jnp.zeros((CHIPS, 128), F32)
    for q in range(Q):
        for g in range(G):
            out_ref[pl.ds(q * 8 + g, CHIPS, stride=48), :] = y[q * CHIPS : (q + 1) * CHIPS, g * 128 : (g + 1) * 128]
        out_ref[pl.ds(q * 8 + G, CHIPS, stride=48), :] = zero


def middle_kernel(
    core_ref, own_ref, oth_ref, kern_ref, swap_ref, table_hbm,
    out_ref, u_ref, l4_ref, even_ref, odd_ref, turn_ref, code_ref, t1_ref, a2_ref, d3_ref, s3_ref, t4_ref, sems,
):
    fetches = []
    row = 0
    targets = [t1_ref.at[i] for i in range(3)]
    for ref in (a2_ref, d3_ref, s3_ref):
        targets += [ref.at[:, k * 384 : (k + 1) * 384] for k in range(3)]
    targets += [t4_ref.at[i] for i in range(3)]
    for k, target in enumerate(targets):
        rows = target.shape[0]
        fetches.append(pltpu.make_async_copy(table_hbm.at[row : row + rows], target, sems.at[k]))
        fetches[-1].start()
        row += rows
    core = core_ref[0]
    mine = core == 0
    lane = lax.broadcasted_iota(jnp.int32, (1, 128), 1)

    pieces = []
    for z in range(ZS):
        a = own_ref[:, z, 0:40, :].reshape(ROWS * 40, 128)
        b = oth_ref[:, z, 0:40, :].reshape(ROWS * 40, 128)
        pieces.append(jnp.where(mine, a, b))
        pieces.append(jnp.where(mine, b, a))
    for i in range(3):
        cols = []
        for v in range(3):
            part = [pieces[3 * v + (k - i) % 3] if 3 * v + (k - i) % 3 < 8 else None for k in range(3)]
            total = part[0] if part[0] is not None else part[1]
            for k in range(1, 3):
                if part[k] is not None and part[k] is not total:
                    total = jnp.where(lane >= k * BV, part[k], total)
            cols.append(total)
        fetches[i].wait()
        u_ref[i] = dot(lhs_split(jnp.concatenate(cols, axis=1)), t1_ref[i]).reshape(ROWS, Q, 8, 384)

    ca, cb = swap_ref[0:1, :], swap_ref[1:2, :]

    def keep(f, q, y):
        for i in range(3):
            l4_ref[i, f * Q + q] = y[i * 128 : (i + 1) * 128]

    for fetch in fetches[3:12]:
        fetch.wait()
    for pair in ((0, 1), (2, 3), (4,)):
        rhs = []
        for q in pair:
            parts = [u_ref[i, :, q, :, :].reshape(ROWS * 8, 384) for i in range(3)]
            rhs.append(rhs_split(jnp.concatenate(parts, axis=0)))
        analysed = dot(a2_ref[...], jnp.concatenate(rhs, axis=1))
        plains = []
        for k, q in enumerate(pair):
            value = analysed[:, k * 384 : (k + 1) * 384] * kern_ref[q]
            swapped = []
            for v in range(3):
                at = slice(v * 128, (v + 1) * 128)
                part = value[:, at]
                swapped.append(pltpu.roll(part, 127, 1) * ca[:, at] + pltpu.roll(part, 1, 1) * cb[:, at])
            plains.append(rhs_split(value))
            turned_rhs = rhs_split(jnp.concatenate(swapped, axis=1))
            y = dot(s3_ref[:, : 3 * N], jnp.concatenate([turned_rhs, plains[-1]], axis=1))
            keep(1, q, y[:, :384])
            keep(2, q, y[:, 384:])
        y = dot(d3_ref[:, : 3 * N], jnp.concatenate(plains, axis=1))
        for k, q in enumerate(pair):
            keep(0, q, y[:, k * 384 : (k + 1) * 384])

    def sort_codes(r, carry):
        for zc in range(8):
            z, c = zc // 2, zc % 2
            blk = jnp.where(core == c, own_ref[r, z, 40:48, :], oth_ref[r, z, 40:48, :])
            code_ref[pl.ds(r * 32 + zc, 4, stride=8), :] = jnp.where(mine, blk[0:4], blk[4:8]).astype(jnp.int32)
        return carry

    lax.fori_loop(0, ROWS, sort_codes, 0)

    def lines_of(k, ref):
        at = pl.ds(pl.multiple_of(k * RR * 8, RR * 8), RR * 8)
        ys = []
        for i in range(3):
            value = l4_ref[i, :, at, :].reshape(FQ * RR * 8, 384)
            ys.append(dot(mix_split(value), t4_ref[i]).reshape(FQ, RR * 8, 384))
            yield
        for zc in range(8):
            v, w = zc // 3, zc % 3
            total = None
            for k3 in range(3):
                part = ys[(k3 - w) % 3][:, :, v * 128 : (v + 1) * 128]
                total = part if total is None else jnp.where(lane >= k3 * BV, part, total)
            for rr in range(RR):
                ref[rr, pl.ds(zc, FQ * 8, stride=8), :] = total[:, rr * 8 : rr * 8 + 8].reshape(FQ * 8, 128)
            if zc % 2:
                yield

    def pick(k, ref):
        for rr in range(RR):
            for d in range(4):
                r = RR * k + rr
                idx = code_ref[pl.ds(pl.multiple_of(r * 32 + d * 8, 8), 8), :]
                at, group = idx & 127, idx >> 7
                here = [group == g for g in range(G)]
                for pf in range(FQ):
                    acc = jnp.zeros((8, 128), F32)
                    for g in range(G):
                        part = ref[rr, (pf * 8 + g) * 8 : (pf * 8 + g) * 8 + 8, :]
                        acc = jnp.where(here[g], jnp.take_along_axis(part, at, axis=1), acc)
                    turn_ref[d, pl.ds(pl.multiple_of(pf * 128 + r * 8, 8), 8), :] = acc
                yield

    def together(*works):
        works = list(works)
        while works:
            works = [w for w in works if next(w, 0) is None]

    steps = ROWS // RR
    for fetch in fetches[12:]:
        fetch.wait()
    together(lines_of(0, even_ref))

    def two(k, carry):
        together(lines_of(2 * k + 1, odd_ref), pick(2 * k, even_ref))
        together(lines_of(2 * k + 2, even_ref), pick(2 * k + 1, odd_ref))
        return carry

    lax.fori_loop(0, steps // 2 - 1, two, 0)
    together(lines_of(steps - 1, odd_ref), pick(steps - 2, even_ref))
    together(pick(steps - 1, odd_ref))

    def turned(pf, carry):
        for d in range(4):
            block = jnp.transpose(turn_ref[d, pl.ds(pl.multiple_of(pf * 128, 128), 128), :])
            for c in range(16):
                at = pl.multiple_of((d * 16 + c) * 8 * FQ + pf * 8, 8)
                out_ref[pl.ds(at, 8), :] = block[c * 8 : c * 8 + 8]
        return carry

    lax.fori_loop(0, FQ, turned, 0, unroll=5)


def last_kernel(x_ref, s5_ref, d5_ref, out_ref):
    k = pl.program_id(0)

    def load(slot, f):
        parts = [x_ref[pl.ds((f * Q + q) * 8 + slot, CHIPS, stride=8 * FQ), :] for q in range(Q)]
        return jnp.concatenate(parts, axis=0)

    for e in range(2):
        both = rhs_split(jnp.concatenate([load(2 * k + e, 0), load(2 * k + e, 1)], axis=1))
        y = dot(s5_ref[...], both)
        out_ref[e, 0] = y[:, 0:128]
        out_ref[e, 1] = y[:, 128:256]
    both = rhs_split(jnp.concatenate([load(2 * k, 2), load(2 * k + 1, 2)], axis=1))
    y = dot(d5_ref[...], both)
    out_ref[0, 2] = y[:, 0:128]
    out_ref[1, 2] = y[:, 128:256]


VM = pl.BlockSpec(memory_space=pltpu.VMEM)
SM = pl.BlockSpec(memory_space=pltpu.SMEM)
HB = pl.BlockSpec(memory_space=pltpu.HBM)


def params(mib):
    return pltpu.CompilerParams(vmem_limit_bytes=mib * 2**20)


def first_call(turn, x, owner, table):
    return pl.pallas_call(
        first_kernel,
        out_shape=jax.ShapeDtypeStruct((CHIPS * 48, 128), F32),
        in_specs=[SM, HB, VM, HB],
        out_specs=VM,
        scratch_shapes=[
            pltpu.VMEM(x.shape, F32),
            pltpu.VMEM(table.shape, BF16),
            pltpu.SemaphoreType.DMA((2,)),
        ],
        compiler_params=params(60),
    )(turn, x, owner, table)


def middle_call(core, own, oth, kern, t):
    shapes = ((3, 1152, 384), (N, 1152), (384, 1152), (384, 1152), (3, 1024, 384))
    return pl.pallas_call(
        middle_kernel,
        out_shape=jax.ShapeDtypeStruct((CHIPS * 8 * FQ, 128), F32),
        in_specs=[SM] + [VM] * 4 + [HB],
        out_specs=VM,
        scratch_shapes=[
            pltpu.VMEM((3, ROWS, Q, 8, 384), F32),
            pltpu.VMEM((3, FQ, 128, 384), F32),
            pltpu.VMEM((RR, FQ * 64, 128), F32),
            pltpu.VMEM((RR, FQ * 64, 128), F32),
            pltpu.VMEM((4, FQ * 128, 128), F32),
            pltpu.VMEM((ROWS * 32, 128), jnp.int32),
        ]
        + [pltpu.VMEM(shape, BF16) for shape in shapes]
        + [pltpu.SemaphoreType.DMA((15,))],
        compiler_params=params(42),
    )(core, own, oth, kern, t["swap"], t["middle"])


def last_call(x, s5, d5):
    return pl.pallas_call(
        last_kernel,
        grid=(4,),
        out_shape=jax.ShapeDtypeStruct((8, 3, N, 128), F32),
        in_specs=[VM] * 3,
        out_specs=pl.BlockSpec((2, 3, N, 128), lambda k: (k, 0, 0, 0)),
        compiler_params=params(32),
    )(x, s5, d5)


def filter_table(chip):
    def wave(p):
        return (p // 2).astype(F32) * STEP

    ka = wave(chip * Q + lax.iota(jnp.int32, Q))[:, None, None]
    kb = wave(lax.iota(jnp.int32, N))[None, :, None]
    kc = wave(lax.iota(jnp.int32, 384))[None, None, :]
    k2 = ka * ka + kb * kb + kc * kc
    off = (k2 <= 0.0) | (lax.iota(jnp.int32, 384)[None, None, :] >= N)
    safe = jnp.where(off, 1.0, k2)
    return jnp.where(off, 0.0, GAIN * safe ** (-0.75) / (1.0 + safe))


def local(noise, owners):
    t = make_tables()
    x = noise.transpose(1, 2, 0).reshape(LINES, N)
    owner = owners.reshape(1, LINES)
    core = lax.axis_index("core").astype(jnp.int32).reshape(1)
    turn = (lax.axis_index("z").astype(jnp.int32) * CORES + core) % 3
    sent = first_call(turn, x, owner, t["first"]).reshape(CHIPS, 48, 128)
    own = lax.all_to_all(sent, ("row", "z"), split_axis=0, concat_axis=0, tiled=True)
    oth = lax.ppermute(own, "core", [(0, 1), (1, 0)])
    chip = lax.axis_index("row") * ZS + lax.axis_index("z")
    shape = (ROWS, ZS, 48, 128)
    slots = middle_call(core, own.reshape(shape), oth.reshape(shape), filter_table(chip), t)
    got = lax.all_to_all(slots.reshape(CHIPS, 8 * FQ, 128), ("row", "z"), split_axis=0, concat_axis=0, tiled=True)
    out = last_call(got.reshape(CHIPS * 8 * FQ, 128), t["s5"], t["d5"])
    return out.reshape(2, 4, 3, N, 128).transpose(4, 0, 1, 2, 3)[None]


def solution(mesh):
    fine = Mesh(mesh.devices.reshape(ROWS, ZS, CORES), ("row", "z", "core"))
    every = ("row", "z", "core")
    in_specs = (P(None, "row", ("z", "core")), P(every, None, None))
    out_specs = P(every, None, None, None, None, None)
    return jax.shard_map(local, mesh=fine, in_specs=in_specs, out_specs=out_specs, check_vma=False)
```

```python
import math

import jax
import jax.numpy as jnp
import ml_dtypes
import numpy as np
from jax import lax
from jax.experimental import pallas as pl
from jax.experimental.pallas import tpu as pltpu
from jax.sharding import Mesh
from jax.sharding import PartitionSpec as P

N = 320
GAIN = 6.0
ROWS, ZS, CORES = 16, 4, 2
CHIPS = ROWS * ZS
BU, BV = 20, 40
Q = 5
CH = 48
FQ = 3 * Q
RR = 2
SP = 4
G = 7
LINES = BU * BV
EMPTY = G * 128
F32, BF16 = jnp.float32, jnp.bfloat16
STEP = 2.0 * math.pi / N


def basis():
    m = np.arange(N // 2)
    x = np.arange(N)
    angle = 2.0 * np.pi / N * (np.outer(m, x) % N)
    kw = (2.0 * np.pi / N * m)[:, None]
    weight = np.where(m == 0, 1.0, 2.0)[:, None] / N
    ana = np.zeros((N, N))
    syn = np.zeros((N, N))
    der = np.zeros((N, N))
    ana[0::2], ana[1::2] = np.cos(angle), np.sin(angle)
    syn[0::2], syn[1::2] = weight * np.cos(angle), weight * np.sin(angle)
    der[0::2], der[1::2] = -weight * kw * np.sin(angle), weight * kw * np.cos(angle)
    return ana, syn.T.copy(), der.T.copy()


def split_np(table):
    hi = table.astype(np.float32).astype(ml_dtypes.bfloat16)
    lo = (table - hi.astype(np.float64)).astype(np.float32).astype(ml_dtypes.bfloat16)
    return hi, lo


def lhs_table(table):
    hi, lo = split_np(table)
    return np.concatenate([hi, lo, hi], axis=1)


def rhs_table(table):
    hi, lo = split_np(table)
    return np.concatenate([hi, hi, lo], axis=0)


def mix_table(table):
    hi, lo = split_np(table)
    return np.concatenate([hi[:256], hi[:256], lo[:256], hi[256:320], hi[256:320], lo[256:384]], axis=0)


def make_tables():
    ana, syn, der = basis()
    third = np.arange(N)
    block, offset = third // BV, third % BV
    places = [(block // 3) * 128 + ((block + i) % 3) * BV + offset for i in range(3)]
    first = ana.reshape(CHIPS, Q, N).transpose(1, 0, 2).reshape(N, N)
    t1 = np.zeros((3, 384, 384))
    t4 = np.zeros((3, 384, 384))
    for i in range(3):
        t1[i, places[i], :N] = ana.T
        t4[i][:N, places[i]] = syn.T
    a2 = np.zeros((N, 3, ROWS, 8))
    s3 = np.zeros((3, ROWS, 8, N))
    d3 = np.zeros((3, ROWS, 8, N))
    for i in range(3):
        for g in range(G):
            u = 3 * g + i
            if u < BU:
                at = np.arange(ROWS) * BU + u
                a2[:, i, :, g] = ana[:, at]
                s3[i, :, g] = syn[at]
                d3[i, :, g] = der[at]
    s5 = syn.reshape(N, CHIPS, Q).transpose(0, 2, 1).reshape(N, N)
    d5 = der.reshape(N, CHIPS, Q).transpose(0, 2, 1).reshape(N, N)
    m = np.arange(384) // 2
    kw = np.where(m < N // 2, 2.0 * np.pi / N * m, 0.0)
    even = np.arange(384) % 2 == 0
    swap = np.zeros((8, 384), np.float32)
    swap[0], swap[1] = np.where(even, kw, 0.0), np.where(even, 0.0, -kw)
    def wide(table):
        table = np.pad(lhs_table(table), ((0, 0), (0, 1152)))
        return [table[:, k * 384 : (k + 1) * 384] for k in range(3)]

    blocks = [rhs_table(t) for t in t1]
    for table in (a2.reshape(N, 384), d3.reshape(384, N), s3.reshape(384, N)):
        blocks += wide(table)
    blocks += [mix_table(t) for t in t4]
    return dict(
        first=lhs_table(first),
        middle=np.concatenate(blocks, axis=0),
        s5=lhs_table(s5),
        d5=lhs_table(d5),
        swap=swap,
    )


def split(value):
    hi = value.astype(BF16)
    return hi, (value - hi.astype(F32)).astype(BF16)


def rhs_split(value):
    hi, lo = split(value)
    return jnp.concatenate([hi, hi, lo], axis=0)


def lhs_split(value):
    hi, lo = split(value)
    return jnp.concatenate([hi, lo, hi], axis=1)


def mix_split(value):
    hi, lo = split(value[:, :256])
    tail = value[:, 256:]
    tail_hi = tail.astype(BF16)
    moved = pltpu.roll(tail - tail_hi.astype(F32), 64, 1)
    lane = lax.broadcasted_iota(jnp.int32, (1, 128), 1)
    mixed = jnp.where(lane < 64, tail, moved).astype(BF16)
    return jnp.concatenate([hi, lo, hi, mixed, tail_hi], axis=1)


def dot(a, b):
    return jnp.dot(a, b, preferred_element_type=F32)


def dot_nt(a, b):
    return lax.dot_general(a, b, (((1,), (1,)), ((), ())), preferred_element_type=F32)


def column(row):
    return jnp.transpose(jnp.broadcast_to(row, (128, 128)))


def slot_codes(owner_ref, turn):
    nb = 7
    lane = lax.broadcasted_iota(jnp.int32, (128, 128), 1)
    sub = lax.broadcasted_iota(jnp.int32, (128, 128), 0)
    one = lax.broadcasted_iota(jnp.int32, (1, 128), 1)
    last = jnp.concatenate([owner_ref[:, 768:LINES], jnp.zeros((1, 896 - LINES), jnp.int32)], axis=1)
    rows = [(owner_ref[:, b * 128 : (b + 1) * 128] if b < nb - 1 else last).astype(F32) for b in range(nb)]
    cols = [column(r) for r in rows]
    dests = []
    for b in range(nb):
        rank = jnp.sum(jnp.where((cols[b] == rows[b]) & (sub < lane), 1.0, 0.0), axis=0, keepdims=True)
        for e in range(b):
            rank = rank + jnp.sum(jnp.where(cols[e] == rows[b], 1.0, 0.0), axis=0, keepdims=True)
        owner = rows[b].astype(jnp.int32)
        device = owner >> 1
        dest = (device & 1) * (CHIPS * 8) + (device >> 1) * 8 + (owner & 1) * 4 + rank.astype(jnp.int32)
        dests.append(jnp.where(one + b * 128 < LINES, dest, -1).astype(F32))
    dcols = [column(d) for d in dests]
    values = []
    for b in range(nb):
        j = sub + b * 128
        group = jnp.zeros_like(j)
        for g in range(1, G):
            group = group + jnp.where(j >= g * 120, 1, 0)
        place = j - group * 120 + turn * BV
        place = jnp.where(place >= 120, place - 120, place)
        values.append((group * 128 + place - EMPTY).astype(F32))
    out = []
    for d in range(8):
        want = (lane + d * 128).astype(F32)
        total = jnp.zeros((128, 128), F32)
        for b in range(nb):
            total = total + jnp.where(dcols[b] == want, values[b], 0.0)
        out.append(jnp.sum(total, axis=0, keepdims=True) + float(EMPTY))
    return jnp.concatenate(out, axis=0)


def first_kernel(turn_ref, x_hbm, owner_ref, table_hbm, out_ref, x_ref, table_ref, sems):
    copies = [
        pltpu.make_async_copy(x_hbm, x_ref, sems.at[0]),
        pltpu.make_async_copy(table_hbm, table_ref, sems.at[1]),
    ]
    for copy in copies:
        copy.start()
    turn = turn_ref[0]
    codes = slot_codes(owner_ref, turn)
    for j in range(CHIPS):
        out_ref[pl.ds(j * 48 + 40, 8), :] = codes
    for copy in copies:
        copy.wait()
    parts = []
    for g in range(G):
        for k in range(3):
            i = jnp.where(k >= turn, k - turn, k - turn + 3)
            u = g * 3 + i
            at = pl.multiple_of(jnp.minimum(u, BU - 1) * BV, 8)
            part = x_ref[pl.ds(at, BV), :]
            parts.append(part if g < G - 1 else jnp.where(u < BU, part, 0.0))
        parts.append(jnp.zeros((8, N), F32))
    hi, lo = split(jnp.concatenate(parts, axis=0))
    th, tl = table_ref[:, 0:N], table_ref[:, N : 2 * N]
    y = dot_nt(th, hi) + (dot_nt(th, lo) + dot_nt(tl, hi))
    zero = jnp.zeros((CHIPS, 128), F32)
    for q in range(Q):
        for g in range(G):
            out_ref[pl.ds(q * 8 + g, CHIPS, stride=48), :] = y[q * CHIPS : (q + 1) * CHIPS, g * 128 : (g + 1) * 128]
        out_ref[pl.ds(q * 8 + G, CHIPS, stride=48), :] = zero


def middle_kernel(
    core_ref, own_ref, oth_ref, kern_ref, swap_ref, table_hbm,
    out_ref, u_ref, l4_ref, even_ref, odd_ref, turn_ref, code_ref, t1_ref, a2_ref, d3_ref, s3_ref, t4_ref, sems,
):
    fetches = []
    row = 0
    targets = [t1_ref.at[i] for i in range(3)]
    for ref in (a2_ref, d3_ref, s3_ref):
        targets += [ref.at[:, k * 384 : (k + 1) * 384] for k in range(3)]
    targets += [t4_ref.at[i] for i in range(3)]
    for k, target in enumerate(targets):
        rows = target.shape[0]
        fetches.append(pltpu.make_async_copy(table_hbm.at[row : row + rows], target, sems.at[k]))
        fetches[-1].start()
        row += rows
    core = core_ref[0]
    mine = core == 0
    lane = lax.broadcasted_iota(jnp.int32, (1, 128), 1)

    pieces = []
    for z in range(ZS):
        a = own_ref[:, z, 0:40, :].reshape(ROWS * 40, 128)
        b = oth_ref[:, z, 0:40, :].reshape(ROWS * 40, 128)
        pieces.append(jnp.where(mine, a, b))
        pieces.append(jnp.where(mine, b, a))
    for i in range(3):
        cols = []
        for v in range(3):
            part = [pieces[3 * v + (k - i) % 3] if 3 * v + (k - i) % 3 < 8 else None for k in range(3)]
            total = part[0] if part[0] is not None else part[1]
            for k in range(1, 3):
                if part[k] is not None and part[k] is not total:
                    total = jnp.where(lane >= k * BV, part[k], total)
            cols.append(total)
        fetches[i].wait()
        u_ref[i] = dot(lhs_split(jnp.concatenate(cols, axis=1)), t1_ref[i]).reshape(ROWS, Q, 8, 384)

    ca, cb = swap_ref[0:1, :], swap_ref[1:2, :]

    def keep(f, q, y):
        for i in range(3):
            l4_ref[i, f * Q + q] = y[i * 128 : (i + 1) * 128]

    for fetch in fetches[3:12]:
        fetch.wait()
    for pair in ((0, 1), (2, 3), (4,)):
        rhs = []
        for q in pair:
            parts = [u_ref[i, :, q, :, :].reshape(ROWS * 8, 384) for i in range(3)]
            rhs.append(rhs_split(jnp.concatenate(parts, axis=0)))
        analysed = dot(a2_ref[...], jnp.concatenate(rhs, axis=1))
        plains = []
        for k, q in enumerate(pair):
            value = analysed[:, k * 384 : (k + 1) * 384] * kern_ref[q]
            swapped = []
            for v in range(3):
                at = slice(v * 128, (v + 1) * 128)
                part = value[:, at]
                swapped.append(pltpu.roll(part, 127, 1) * ca[:, at] + pltpu.roll(part, 1, 1) * cb[:, at])
            plains.append(rhs_split(value))
            turned_rhs = rhs_split(jnp.concatenate(swapped, axis=1))
            y = dot(s3_ref[:, : 3 * N], jnp.concatenate([turned_rhs, plains[-1]], axis=1))
            keep(1, q, y[:, :384])
            keep(2, q, y[:, 384:])
        y = dot(d3_ref[:, : 3 * N], jnp.concatenate(plains, axis=1))
        for k, q in enumerate(pair):
            keep(0, q, y[:, k * 384 : (k + 1) * 384])

    def sort_codes(r, carry):
        for zc in range(8):
            z, c = zc // 2, zc % 2
            blk = jnp.where(core == c, own_ref[r, z, 40:48, :], oth_ref[r, z, 40:48, :])
            code_ref[pl.ds(r * 32 + zc, 4, stride=8), :] = jnp.where(mine, blk[0:4], blk[4:8]).astype(jnp.int32)
        return carry

    lax.fori_loop(0, ROWS, sort_codes, 0)

    def lines_of(k, ref):
        at = pl.ds(pl.multiple_of(k * RR * 8, RR * 8), RR * 8)
        ys = []
        for i in range(3):
            value = l4_ref[i, :, at, :].reshape(FQ * RR * 8, 384)
            ys.append(dot(mix_split(value), t4_ref[i]).reshape(FQ, RR * 8, 384))
            yield
        for zc in range(8):
            v, w = zc // 3, zc % 3
            total = None
            for k3 in range(3):
                part = ys[(k3 - w) % 3][:, :, v * 128 : (v + 1) * 128]
                total = part if total is None else jnp.where(lane >= k3 * BV, part, total)
            for rr in range(RR):
                ref[rr, pl.ds(zc, FQ * 8, stride=8), :] = total[:, rr * 8 : rr * 8 + 8].reshape(FQ * 8, 128)
            if zc % 2:
                yield

    def pick(k, ref):
        for rr in range(RR):
            for d in range(4):
                r = RR * k + rr
                idx = code_ref[pl.ds(pl.multiple_of(r * 32 + d * 8, 8), 8), :]
                at, group = idx & 127, idx >> 7
                here = [group == g for g in range(G)]
                for pf in range(FQ):
                    acc = jnp.zeros((8, 128), F32)
                    for g in range(G):
                        part = ref[rr, (pf * 8 + g) * 8 : (pf * 8 + g) * 8 + 8, :]
                        acc = jnp.where(here[g], jnp.take_along_axis(part, at, axis=1), acc)
                    turn_ref[d, pl.ds(pl.multiple_of(pf * 128 + r * 8, 8), 8), :] = acc
                yield

    def together(*works):
        works = list(works)
        while works:
            works = [w for w in works if next(w, 0) is None]

    steps = ROWS // RR
    for fetch in fetches[12:]:
        fetch.wait()
    together(lines_of(0, even_ref))

    def two(k, carry):
        together(lines_of(2 * k + 1, odd_ref), pick(2 * k, even_ref))
        together(lines_of(2 * k + 2, even_ref), pick(2 * k + 1, odd_ref))
        return carry

    lax.fori_loop(0, steps // 2 - 1, two, 0)
    together(lines_of(steps - 1, odd_ref), pick(steps - 2, even_ref))
    together(pick(steps - 1, odd_ref))

    def turned(pf, carry):
        for d in range(4):
            block = jnp.transpose(turn_ref[d, pl.ds(pl.multiple_of(pf * 128, 128), 128), :])
            for c in range(16):
                at = pl.multiple_of((d * 16 + c) * 8 * FQ + pf * 8, 8)
                out_ref[pl.ds(at, 8), :] = block[c * 8 : c * 8 + 8]
        return carry

    lax.fori_loop(0, FQ, turned, 0, unroll=5)


def last_kernel(x_ref, s5_ref, d5_ref, out_ref):
    first = pl.program_id(0) * SP

    def load(slot, f):
        parts = [x_ref[pl.ds((f * Q + q) * 8 + slot, CHIPS, stride=8 * FQ), :] for q in range(Q)]
        return jnp.concatenate(parts, axis=0)

    for e in range(0, SP, 2):
        for slot in (e, e + 1):
            both = rhs_split(jnp.concatenate([load(first + slot, 0), load(first + slot, 1)], axis=1))
            y = dot(s5_ref[...], both)
            out_ref[slot, 0] = y[:, 0:128]
            out_ref[slot, 1] = y[:, 128:256]
        both = rhs_split(jnp.concatenate([load(first + e, 2), load(first + e + 1, 2)], axis=1))
        y = dot(d5_ref[...], both)
        out_ref[e, 2] = y[:, 0:128]
        out_ref[e + 1, 2] = y[:, 128:256]


VM = pl.BlockSpec(memory_space=pltpu.VMEM)
SM = pl.BlockSpec(memory_space=pltpu.SMEM)
HB = pl.BlockSpec(memory_space=pltpu.HBM)


def params(mib):
    return pltpu.CompilerParams(vmem_limit_bytes=mib * 2**20)


def first_call(turn, x, owner, table):
    return pl.pallas_call(
        first_kernel,
        out_shape=jax.ShapeDtypeStruct((CHIPS * 48, 128), F32),
        in_specs=[SM, HB, VM, HB],
        out_specs=VM,
        scratch_shapes=[
            pltpu.VMEM(x.shape, F32),
            pltpu.VMEM(table.shape, BF16),
            pltpu.SemaphoreType.DMA((2,)),
        ],
        compiler_params=params(60),
    )(turn, x, owner, table)


def middle_call(core, own, oth, kern, t):
    shapes = ((3, 1152, 384), (N, 1152), (384, 1152), (384, 1152), (3, 1024, 384))
    return pl.pallas_call(
        middle_kernel,
        out_shape=jax.ShapeDtypeStruct((CHIPS * 8 * FQ, 128), F32),
        in_specs=[SM] + [VM] * 4 + [HB],
        out_specs=VM,
        scratch_shapes=[
            pltpu.VMEM((3, ROWS, Q, 8, 384), F32),
            pltpu.VMEM((3, FQ, 128, 384), F32),
            pltpu.VMEM((RR, FQ * 64, 128), F32),
            pltpu.VMEM((RR, FQ * 64, 128), F32),
            pltpu.VMEM((4, FQ * 128, 128), F32),
            pltpu.VMEM((ROWS * 32, 128), jnp.int32),
        ]
        + [pltpu.VMEM(shape, BF16) for shape in shapes]
        + [pltpu.SemaphoreType.DMA((15,))],
        compiler_params=params(42),
    )(core, own, oth, kern, t["swap"], t["middle"])


def last_call(x, s5, d5):
    return pl.pallas_call(
        last_kernel,
        grid=(8 // SP,),
        out_shape=jax.ShapeDtypeStruct((8, 3, N, 128), F32),
        in_specs=[VM] * 3,
        out_specs=pl.BlockSpec((SP, 3, N, 128), lambda k: (k, 0, 0, 0)),
        compiler_params=params(32),
    )(x, s5, d5)


def filter_table(chip):
    def wave(p):
        return (p // 2).astype(F32) * STEP

    ka = wave(chip * Q + lax.iota(jnp.int32, Q))[:, None, None]
    kb = wave(lax.iota(jnp.int32, N))[None, :, None]
    kc = wave(lax.iota(jnp.int32, 384))[None, None, :]
    k2 = ka * ka + kb * kb + kc * kc
    off = (k2 <= 0.0) | (lax.iota(jnp.int32, 384)[None, None, :] >= N)
    safe = jnp.where(off, 1.0, k2)
    return jnp.where(off, 0.0, GAIN * safe ** (-0.75) / (1.0 + safe))


def local(noise, owners):
    t = make_tables()
    x = noise.transpose(1, 2, 0).reshape(LINES, N)
    owner = owners.reshape(1, LINES)
    core = lax.axis_index("core").astype(jnp.int32).reshape(1)
    turn = (lax.axis_index("z").astype(jnp.int32) * CORES + core) % 3
    sent = first_call(turn, x, owner, t["first"]).reshape(CHIPS, 48, 128)
    own = lax.all_to_all(sent, ("row", "z"), split_axis=0, concat_axis=0, tiled=True)
    oth = lax.ppermute(own, "core", [(0, 1), (1, 0)])
    chip = lax.axis_index("row") * ZS + lax.axis_index("z")
    shape = (ROWS, ZS, 48, 128)
    slots = middle_call(core, own.reshape(shape), oth.reshape(shape), filter_table(chip), t)
    got = lax.all_to_all(slots.reshape(CHIPS, 8 * FQ, 128), ("row", "z"), split_axis=0, concat_axis=0, tiled=True)
    out = last_call(got.reshape(CHIPS * 8 * FQ, 128), t["s5"], t["d5"])
    return out.reshape(2, 4, 3, N, 128).transpose(4, 0, 1, 2, 3)[None]


def solution(mesh):
    fine = Mesh(mesh.devices.reshape(ROWS, ZS, CORES), ("row", "z", "core"))
    every = ("row", "z", "core")
    in_specs = (P(None, "row", ("z", "core")), P(every, None, None))
    out_specs = P(every, None, None, None, None, None)
    return jax.shard_map(local, mesh=fine, in_specs=in_specs, out_specs=out_specs, check_vma=False)
```

```python
import math

import jax
import jax.numpy as jnp
import ml_dtypes
import numpy as np
from jax import lax
from jax.experimental import pallas as pl
from jax.experimental.pallas import tpu as pltpu
from jax.sharding import Mesh
from jax.sharding import PartitionSpec as P

N = 320
GAIN = 6.0
ROWS, ZS, CORES = 16, 4, 2
CHIPS = ROWS * ZS
BU, BV = 20, 40
Q = 5
CH = 48
FQ = 3 * Q
RR = 2
SP = 4
G = 7
LINES = BU * BV
EMPTY = G * 128
F32, BF16 = jnp.float32, jnp.bfloat16
STEP = 2.0 * math.pi / N


def basis():
    m = np.arange(N // 2)
    x = np.arange(N)
    angle = 2.0 * np.pi / N * (np.outer(m, x) % N)
    kw = (2.0 * np.pi / N * m)[:, None]
    weight = np.where(m == 0, 1.0, 2.0)[:, None] / N
    ana = np.zeros((N, N))
    syn = np.zeros((N, N))
    der = np.zeros((N, N))
    ana[0::2], ana[1::2] = np.cos(angle), np.sin(angle)
    syn[0::2], syn[1::2] = weight * np.cos(angle), weight * np.sin(angle)
    der[0::2], der[1::2] = -weight * kw * np.sin(angle), weight * kw * np.cos(angle)
    return ana, syn.T.copy(), der.T.copy()


def split_np(table):
    hi = table.astype(np.float32).astype(ml_dtypes.bfloat16)
    lo = (table - hi.astype(np.float64)).astype(np.float32).astype(ml_dtypes.bfloat16)
    return hi, lo


def lhs_table(table):
    hi, lo = split_np(table)
    return np.concatenate([hi, lo, hi], axis=1)


def rhs_table(table):
    hi, lo = split_np(table)
    return np.concatenate([hi, hi, lo], axis=0)


def mix_table(table):
    hi, lo = split_np(table)
    return np.concatenate([hi[:256], hi[:256], lo[:256], hi[256:320], hi[256:320], lo[256:384]], axis=0)


def make_tables():
    ana, syn, der = basis()
    third = np.arange(N)
    block, offset = third // BV, third % BV
    places = [(block // 3) * 128 + ((block + i) % 3) * BV + offset for i in range(3)]
    first = ana.reshape(CHIPS, Q, N).transpose(1, 0, 2).reshape(N, N)
    t1 = np.zeros((3, 384, 384))
    t4 = np.zeros((3, 384, 384))
    for i in range(3):
        t1[i, places[i], :N] = ana.T
        t4[i][:N, places[i]] = syn.T
    a2 = np.zeros((N, 3, ROWS, 8))
    s3 = np.zeros((3, ROWS, 8, N))
    d3 = np.zeros((3, ROWS, 8, N))
    for i in range(3):
        for g in range(G):
            u = 3 * g + i
            if u < BU:
                at = np.arange(ROWS) * BU + u
                a2[:, i, :, g] = ana[:, at]
                s3[i, :, g] = syn[at]
                d3[i, :, g] = der[at]
    s5 = syn.reshape(N, CHIPS, Q).transpose(0, 2, 1).reshape(N, N)
    d5 = der.reshape(N, CHIPS, Q).transpose(0, 2, 1).reshape(N, N)
    m = np.arange(384) // 2
    kw = np.where(m < N // 2, 2.0 * np.pi / N * m, 0.0)
    even = np.arange(384) % 2 == 0
    swap = np.zeros((8, 384), np.float32)
    swap[0], swap[1] = np.where(even, kw, 0.0), np.where(even, 0.0, -kw)
    def wide(table):
        table = np.pad(lhs_table(table), ((0, 0), (0, 1152)))
        return [table[:, k * 384 : (k + 1) * 384] for k in range(3)]

    blocks = [rhs_table(t) for t in t1]
    for table in (a2.reshape(N, 384), d3.reshape(384, N), s3.reshape(384, N)):
        blocks += wide(table)
    blocks += [mix_table(t) for t in t4]
    return dict(
        first=lhs_table(first),
        middle=np.concatenate(blocks, axis=0),
        s5=lhs_table(s5),
        d5=lhs_table(d5),
        swap=swap,
    )


def split(value):
    hi = value.astype(BF16)
    return hi, (value - hi.astype(F32)).astype(BF16)


def rhs_split(value):
    hi, lo = split(value)
    return jnp.concatenate([hi, hi, lo], axis=0)


def lhs_split(value):
    hi, lo = split(value)
    return jnp.concatenate([hi, lo, hi], axis=1)


def mix_split(value):
    hi, lo = split(value[:, :256])
    tail = value[:, 256:]
    tail_hi = tail.astype(BF16)
    moved = pltpu.roll(tail - tail_hi.astype(F32), 64, 1)
    lane = lax.broadcasted_iota(jnp.int32, (1, 128), 1)
    mixed = jnp.where(lane < 64, tail, moved).astype(BF16)
    return jnp.concatenate([hi, lo, hi, mixed, tail_hi], axis=1)


def dot(a, b):
    return jnp.dot(a, b, preferred_element_type=F32)


def dot_nt(a, b):
    return lax.dot_general(a, b, (((1,), (1,)), ((), ())), preferred_element_type=F32)


def column(row):
    return jnp.transpose(jnp.broadcast_to(row, (128, 128)))


def slot_codes(owner_ref, turn):
    nb = 7
    lane = lax.broadcasted_iota(jnp.int32, (128, 128), 1)
    sub = lax.broadcasted_iota(jnp.int32, (128, 128), 0)
    one = lax.broadcasted_iota(jnp.int32, (1, 128), 1)
    last = jnp.concatenate([owner_ref[:, 768:LINES], jnp.zeros((1, 896 - LINES), jnp.int32)], axis=1)
    rows = [(owner_ref[:, b * 128 : (b + 1) * 128] if b < nb - 1 else last).astype(F32) for b in range(nb)]
    cols = [column(r) for r in rows]
    dests = []
    for b in range(nb):
        rank = jnp.sum(jnp.where((cols[b] == rows[b]) & (sub < lane), 1.0, 0.0), axis=0, keepdims=True)
        for e in range(b):
            rank = rank + jnp.sum(jnp.where(cols[e] == rows[b], 1.0, 0.0), axis=0, keepdims=True)
        owner = rows[b].astype(jnp.int32)
        device = owner >> 1
        dest = (device & 1) * (CHIPS * 8) + (device >> 1) * 8 + (owner & 1) * 4 + rank.astype(jnp.int32)
        dests.append(jnp.where(one + b * 128 < LINES, dest, -1).astype(F32))
    dcols = [column(d) for d in dests]
    values = []
    for b in range(nb):
        j = sub + b * 128
        group = jnp.zeros_like(j)
        for g in range(1, G):
            group = group + jnp.where(j >= g * 120, 1, 0)
        place = j - group * 120 + turn * BV
        place = jnp.where(place >= 120, place - 120, place)
        values.append((group * 128 + place - EMPTY).astype(F32))
    out = []
    for d in range(8):
        want = (lane + d * 128).astype(F32)
        total = jnp.zeros((128, 128), F32)
        for b in range(nb):
            total = total + jnp.where(dcols[b] == want, values[b], 0.0)
        out.append(jnp.sum(total, axis=0, keepdims=True) + float(EMPTY))
    return jnp.concatenate(out, axis=0)


def first_kernel(turn_ref, x_hbm, owner_ref, table_hbm, out_ref, x_ref, table_ref, sems):
    copies = [
        pltpu.make_async_copy(x_hbm, x_ref, sems.at[0]),
        pltpu.make_async_copy(table_hbm, table_ref, sems.at[1]),
    ]
    for copy in copies:
        copy.start()
    turn = turn_ref[0]
    codes = slot_codes(owner_ref, turn)
    for j in range(CHIPS):
        out_ref[pl.ds(j * 48 + 40, 8), :] = codes
    for copy in copies:
        copy.wait()
    parts = []
    for g in range(G):
        for k in range(3):
            i = jnp.where(k >= turn, k - turn, k - turn + 3)
            u = g * 3 + i
            at = pl.multiple_of(jnp.minimum(u, BU - 1) * BV, 8)
            part = x_ref[pl.ds(at, BV), :]
            parts.append(part if g < G - 1 else jnp.where(u < BU, part, 0.0))
        parts.append(jnp.zeros((8, N), F32))
    hi, lo = split(jnp.concatenate(parts, axis=0))
    th, tl = table_ref[:, 0:N], table_ref[:, N : 2 * N]
    y = dot_nt(th, hi) + (dot_nt(th, lo) + dot_nt(tl, hi))
    zero = jnp.zeros((CHIPS, 128), F32)
    for q in range(Q):
        for g in range(G):
            out_ref[pl.ds(q * 8 + g, CHIPS, stride=48), :] = y[q * CHIPS : (q + 1) * CHIPS, g * 128 : (g + 1) * 128]
        out_ref[pl.ds(q * 8 + G, CHIPS, stride=48), :] = zero


def middle_kernel(
    core_ref, own_ref, oth_ref, kern_ref, swap_ref, table_hbm,
    out_ref, u_ref, l4_ref, even_ref, odd_ref, turn_ref, code_ref, t1_ref, a2_ref, d3_ref, s3_ref, t4_ref, sems,
):
    fetches = []
    row = 0
    targets = [t1_ref.at[i] for i in range(3)]
    for ref in (a2_ref, d3_ref, s3_ref):
        targets += [ref.at[:, k * 384 : (k + 1) * 384] for k in range(3)]
    targets += [t4_ref.at[i] for i in range(3)]
    for k, target in enumerate(targets):
        rows = target.shape[0]
        fetches.append(pltpu.make_async_copy(table_hbm.at[row : row + rows], target, sems.at[k]))
        fetches[-1].start()
        row += rows
    core = core_ref[0]
    mine = core == 0
    lane = lax.broadcasted_iota(jnp.int32, (1, 128), 1)

    def sort_codes(r, carry):
        for zc in range(8):
            z, c = zc // 2, zc % 2
            blk = jnp.where(core == c, own_ref[r, z, 40:48, :], oth_ref[r, z, 40:48, :])
            code_ref[pl.ds(r * 32 + zc, 4, stride=8), :] = jnp.where(mine, blk[0:4], blk[4:8]).astype(jnp.int32)
        return carry

    lax.fori_loop(0, ROWS, sort_codes, 0)

    pieces = []
    for z in range(ZS):
        a = own_ref[:, z, 0:40, :].reshape(ROWS * 40, 128)
        b = oth_ref[:, z, 0:40, :].reshape(ROWS * 40, 128)
        pieces.append(jnp.where(mine, a, b))
        pieces.append(jnp.where(mine, b, a))
    for i in range(3):
        cols = []
        for v in range(3):
            part = [pieces[3 * v + (k - i) % 3] if 3 * v + (k - i) % 3 < 8 else None for k in range(3)]
            total = part[0] if part[0] is not None else part[1]
            for k in range(1, 3):
                if part[k] is not None and part[k] is not total:
                    total = jnp.where(lane >= k * BV, part[k], total)
            cols.append(total)
        fetches[i].wait()
        u_ref[i] = dot(lhs_split(jnp.concatenate(cols, axis=1)), t1_ref[i]).reshape(ROWS, Q, 8, 384)

    ca, cb = swap_ref[0:1, :], swap_ref[1:2, :]

    def keep(f, q, y):
        for i in range(3):
            l4_ref[i, f * Q + q] = y[i * 128 : (i + 1) * 128]

    for fetch in fetches[3:12]:
        fetch.wait()
    for pair in ((0, 1), (2, 3), (4,)):
        rhs = []
        for q in pair:
            parts = [u_ref[i, :, q, :, :].reshape(ROWS * 8, 384) for i in range(3)]
            rhs.append(rhs_split(jnp.concatenate(parts, axis=0)))
        analysed = dot(a2_ref[...], jnp.concatenate(rhs, axis=1))
        plains = []
        for k, q in enumerate(pair):
            value = analysed[:, k * 384 : (k + 1) * 384] * kern_ref[q]
            swapped = []
            for v in range(3):
                at = slice(v * 128, (v + 1) * 128)
                part = value[:, at]
                swapped.append(pltpu.roll(part, 127, 1) * ca[:, at] + pltpu.roll(part, 1, 1) * cb[:, at])
            plains.append(rhs_split(value))
            turned_rhs = rhs_split(jnp.concatenate(swapped, axis=1))
            y = dot(s3_ref[:, : 3 * N], jnp.concatenate([turned_rhs, plains[-1]], axis=1))
            keep(1, q, y[:, :384])
            keep(2, q, y[:, 384:])
        y = dot(d3_ref[:, : 3 * N], jnp.concatenate(plains, axis=1))
        for k, q in enumerate(pair):
            keep(0, q, y[:, k * 384 : (k + 1) * 384])

    def lines_of(k, ref):
        at = pl.ds(pl.multiple_of(k * RR * 8, RR * 8), RR * 8)
        ys = []
        for i in range(3):
            value = l4_ref[i, :, at, :].reshape(FQ * RR * 8, 384)
            ys.append(dot(mix_split(value), t4_ref[i]).reshape(FQ, RR * 8, 384))
            yield
        for zc in range(8):
            v, w = zc // 3, zc % 3
            total = None
            for k3 in range(3):
                part = ys[(k3 - w) % 3][:, :, v * 128 : (v + 1) * 128]
                total = part if total is None else jnp.where(lane >= k3 * BV, part, total)
            for rr in range(RR):
                ref[rr, pl.ds(zc, FQ * 8, stride=8), :] = total[:, rr * 8 : rr * 8 + 8].reshape(FQ * 8, 128)
            if zc % 2:
                yield

    def pick(k, ref):
        for rr in range(RR):
            for d in range(4):
                r = RR * k + rr
                idx = code_ref[pl.ds(pl.multiple_of(r * 32 + d * 8, 8), 8), :]
                at, group = idx & 127, idx >> 7
                here = [group == g for g in range(G)]
                for pf in range(FQ):
                    acc = jnp.zeros((8, 128), F32)
                    for g in range(G):
                        part = ref[rr, (pf * 8 + g) * 8 : (pf * 8 + g) * 8 + 8, :]
                        acc = jnp.where(here[g], jnp.take_along_axis(part, at, axis=1), acc)
                    turn_ref[d, pl.ds(pl.multiple_of(pf * 128 + r * 8, 8), 8), :] = acc
                yield

    def together(*works):
        works = list(works)
        while works:
            works = [w for w in works if next(w, 0) is None]

    steps = ROWS // RR
    for fetch in fetches[12:]:
        fetch.wait()
    together(lines_of(0, even_ref))

    def two(k, carry):
        together(lines_of(2 * k + 1, odd_ref), pick(2 * k, even_ref))
        together(lines_of(2 * k + 2, even_ref), pick(2 * k + 1, odd_ref))
        return carry

    lax.fori_loop(0, steps // 2 - 1, two, 0)
    together(lines_of(steps - 1, odd_ref), pick(steps - 2, even_ref))
    together(pick(steps - 1, odd_ref))

    def turned(pf, carry):
        for d in range(4):
            block = jnp.transpose(turn_ref[d, pl.ds(pl.multiple_of(pf * 128, 128), 128), :])
            for c in range(16):
                at = pl.multiple_of((d * 16 + c) * 8 * FQ + pf * 8, 8)
                out_ref[pl.ds(at, 8), :] = block[c * 8 : c * 8 + 8]
        return carry

    lax.fori_loop(0, FQ, turned, 0, unroll=5)


def last_kernel(x_ref, s5_ref, d5_ref, out_ref):
    first = pl.program_id(0) * SP

    def load(slot, f):
        parts = [x_ref[pl.ds((f * Q + q) * 8 + slot, CHIPS, stride=8 * FQ), :] for q in range(Q)]
        return jnp.concatenate(parts, axis=0)

    for e in range(0, SP, 2):
        for slot in (e, e + 1):
            both = rhs_split(jnp.concatenate([load(first + slot, 0), load(first + slot, 1)], axis=1))
            y = dot(s5_ref[...], both)
            out_ref[slot, 0] = y[:, 0:128]
            out_ref[slot, 1] = y[:, 128:256]
        both = rhs_split(jnp.concatenate([load(first + e, 2), load(first + e + 1, 2)], axis=1))
        y = dot(d5_ref[...], both)
        out_ref[e, 2] = y[:, 0:128]
        out_ref[e + 1, 2] = y[:, 128:256]


VM = pl.BlockSpec(memory_space=pltpu.VMEM)
SM = pl.BlockSpec(memory_space=pltpu.SMEM)
HB = pl.BlockSpec(memory_space=pltpu.HBM)


def params(mib):
    return pltpu.CompilerParams(vmem_limit_bytes=mib * 2**20)


def first_call(turn, x, owner, table):
    return pl.pallas_call(
        first_kernel,
        out_shape=jax.ShapeDtypeStruct((CHIPS * 48, 128), F32),
        in_specs=[SM, HB, VM, HB],
        out_specs=VM,
        scratch_shapes=[
            pltpu.VMEM(x.shape, F32),
            pltpu.VMEM(table.shape, BF16),
            pltpu.SemaphoreType.DMA((2,)),
        ],
        compiler_params=params(60),
    )(turn, x, owner, table)


def middle_call(core, own, oth, kern, t):
    shapes = ((3, 1152, 384), (N, 1152), (384, 1152), (384, 1152), (3, 1024, 384))
    return pl.pallas_call(
        middle_kernel,
        out_shape=jax.ShapeDtypeStruct((CHIPS * 8 * FQ, 128), F32),
        in_specs=[SM] + [VM] * 4 + [HB],
        out_specs=VM,
        scratch_shapes=[
            pltpu.VMEM((3, ROWS, Q, 8, 384), F32),
            pltpu.VMEM((3, FQ, 128, 384), F32),
            pltpu.VMEM((RR, FQ * 64, 128), F32),
            pltpu.VMEM((RR, FQ * 64, 128), F32),
            pltpu.VMEM((4, FQ * 128, 128), F32),
            pltpu.VMEM((ROWS * 32, 128), jnp.int32),
        ]
        + [pltpu.VMEM(shape, BF16) for shape in shapes]
        + [pltpu.SemaphoreType.DMA((15,))],
        compiler_params=params(42),
    )(core, own, oth, kern, t["swap"], t["middle"])


def last_call(x, s5, d5):
    return pl.pallas_call(
        last_kernel,
        grid=(8 // SP,),
        out_shape=jax.ShapeDtypeStruct((8, 3, N, 128), F32),
        in_specs=[VM] * 3,
        out_specs=pl.BlockSpec((SP, 3, N, 128), lambda k: (k, 0, 0, 0)),
        compiler_params=params(32),
    )(x, s5, d5)


def filter_table(chip):
    def wave(p):
        return (p // 2).astype(F32) * STEP

    ka = wave(chip * Q + lax.iota(jnp.int32, Q))[:, None, None]
    kb = wave(lax.iota(jnp.int32, N))[None, :, None]
    kc = wave(lax.iota(jnp.int32, 384))[None, None, :]
    k2 = ka * ka + kb * kb + kc * kc
    off = (k2 <= 0.0) | (lax.iota(jnp.int32, 384)[None, None, :] >= N)
    safe = jnp.where(off, 1.0, k2)
    return jnp.where(off, 0.0, GAIN * safe ** (-0.75) / (1.0 + safe))


def local(noise, owners):
    t = make_tables()
    x = noise.transpose(1, 2, 0).reshape(LINES, N)
    owner = owners.reshape(1, LINES)
    core = lax.axis_index("core").astype(jnp.int32).reshape(1)
    turn = (lax.axis_index("z").astype(jnp.int32) * CORES + core) % 3
    sent = first_call(turn, x, owner, t["first"]).reshape(CHIPS, 48, 128)
    own = lax.all_to_all(sent, ("row", "z"), split_axis=0, concat_axis=0, tiled=True)
    oth = lax.ppermute(own, "core", [(0, 1), (1, 0)])
    chip = lax.axis_index("row") * ZS + lax.axis_index("z")
    shape = (ROWS, ZS, 48, 128)
    slots = middle_call(core, own.reshape(shape), oth.reshape(shape), filter_table(chip), t)
    got = lax.all_to_all(slots.reshape(CHIPS, 8 * FQ, 128), ("row", "z"), split_axis=0, concat_axis=0, tiled=True)
    out = last_call(got.reshape(CHIPS * 8 * FQ, 128), t["s5"], t["d5"])
    return out.reshape(2, 4, 3, N, 128).transpose(4, 0, 1, 2, 3)[None]


def solution(mesh):
    fine = Mesh(mesh.devices.reshape(ROWS, ZS, CORES), ("row", "z", "core"))
    every = ("row", "z", "core")
    in_specs = (P(None, "row", ("z", "core")), P(every, None, None))
    out_specs = P(every, None, None, None, None, None)
    return jax.shard_map(local, mesh=fine, in_specs=in_specs, out_specs=out_specs, check_vma=False)
```
